32 devices in a mesh: rows: 16 (over z, y, x), rep: 2 (over core).
Axes of the slice: x: 2, y: 2, z: 4, core: 2. Of those that a mesh axis runs over, the one named last changes fastest.
Arguments:
- nodes: bfloat16 [2048, 512], P('rows'), may hold values from -6 to 6
- adjacency: bfloat16 [2048, 2048], P('rows', 'rep'), may hold values from 0 to 2, as said below
- gain: float32 [512], replicated, may hold values from 0.1 to 1.9
- w_in: bfloat16 [512, 512], replicated, may hold values from -0.25 to 0.25
- w_out: bfloat16 [512, 512], replicated, may hold values from -0.25 to 0.25
- cotangent: bfloat16 [2048, 512], P('rows'), may hold values from -2 to 2
Outputs:
- node_out: bfloat16 [2048, 512], P('rows')
- node_grad: bfloat16 [2048, 512], P('rows')
- grad_w_in: float32 [512, 512], replicated
- grad_w_out: float32 [512, 512], replicated
- grad_gain: float32 [512], replicated
The draws below stay inside these ranges and needn't reach their ends.
Inputs may be any that keep to these rules, and one draw needn't show every extreme that they name: adjacency holds whole numbers, is symmetric, every diagonal entry is 1, and off the diagonal it is zero outside a set of live 128 x 128 blocks.
All inputs are finite; a program needn't handle non-finite values.
Results may differ from the reference program's by a relative error of at most 0.0054.
Values may be sent and summed in bfloat16 or wider, within the bound.
A program may use at most 64 MiB of HBM per device.

```python
import jax
import jax.numpy as jnp
from jax import lax

D = 512
BLOCK = 128
GROUP_ROWS = 128
NODES = 2048
N_ROWS = 16


def draw_adjacency(key, part):
    key = jax.random.fold_in(key, 11)
    key_hot, key_live, key_seed = jax.random.split(key, 3)
    blocks = NODES // BLOCK
    hotness = jax.random.randint(key_hot, (blocks,), 1, 6)
    chance = jax.random.randint(key_live, (blocks, blocks), 0, 160)
    chance = jnp.minimum(chance, chance.T)
    block_ids = jnp.arange(blocks, dtype=jnp.int32)
    live = (chance < hotness[:, None] * hotness[None, :]) | (jnp.abs(block_ids[:, None] - block_ids[None, :]) <= 1)
    live_full = jnp.repeat(jnp.repeat(live, BLOCK, axis=0), BLOCK, axis=1)
    seed_value = jax.random.randint(key_seed, (), 0, 1048576)
    index = jnp.arange(NODES, dtype=jnp.int32)
    product = index[:, None] * index[None, :]
    total = index[:, None] + index[None, :]
    mixed = product * 40503 + total * 9973 + seed_value
    mixed = jnp.bitwise_xor(mixed, jnp.right_shift(mixed, 15))
    mixed = mixed * 2246822
    mixed = jnp.bitwise_xor(mixed, jnp.right_shift(mixed, 13))
    pattern = jnp.bitwise_and(jnp.right_shift(mixed, 4), 15)
    multiple = jnp.where(pattern == 0, 2.0, jnp.where(pattern < 3, 1.0, 0.0))
    multiple = jnp.where(live_full, multiple, 0.0)
    diagonal = index[:, None] == index[None, :]
    return jnp.where(diagonal, 1.0, multiple).astype(jnp.float32).astype(jnp.bfloat16)


def level_of(own_key, dims, cuts, least, largest):
    def one(dim, blocks):
        steps = jax.random.uniform(jax.random.fold_in(jax.random.fold_in(own_key, 6), dim), (blocks,), jnp.float32, least / len(cuts), largest / len(cuts))
        return jnp.repeat(jnp.exp(steps), dims[dim] // blocks).reshape((-1,) + (1,) * (len(dims) - dim - 1))

    level = one(*cuts[0])
    for cut in cuts[1:]:
        level = level * one(*cut)
    return level


def noise(stream_key, dims, deviation, limit, shards=(), held_as=jnp.bfloat16):
    loudness = level_of(stream_key, dims, shards, -0.22, 0.18) if shards else 1.0
    result = jax.random.normal(stream_key, dims, jnp.float32) * deviation * loudness
    return jnp.minimum(jnp.maximum(result, -limit), limit).astype(held_as)


def setup_inputs(seed: int = 0) -> dict:
    arg_keys = jax.random.split(jax.random.key(seed), 7)
    return {
        "nodes": noise(arg_keys[0], (NODES, D), 1.0, 6.0, ((0, 16),)),
        "adjacency": draw_adjacency(jax.random.fold_in(arg_keys[6], 71), 0),
        "gain": jnp.clip(1.0 + 0.18 * jax.random.normal(arg_keys[2], (D,), jnp.float32), 0.1, 1.9),
        "w_in": noise(arg_keys[3], (D, D), D ** -0.5, 0.25),
        "w_out": noise(arg_keys[4], (D, D), D ** -0.5, 0.25),
        "cotangent": noise(arg_keys[5], (NODES, D), 0.125, 2.0, ((0, 16),)),
    }


def aggregate(adjacency, field):
    field_wide = field.astype(jnp.float32)
    slabs = adjacency.reshape(N_ROWS, GROUP_ROWS, NODES)

    def one_slab(slab):
        return jnp.dot(slab.astype(jnp.float32), field_wide, precision=lax.Precision.HIGHEST)
    return lax.map(one_slab, slabs).reshape(NODES, field.shape[1])

def reference(nodes, adjacency, gain, w_in, w_out, cotangent):
    summed = aggregate(adjacency, nodes)
    scale = lax.rsqrt(lax.optimization_barrier(jnp.mean(summed * summed, axis=-1, keepdims=True)) + 1e-05)
    normed = summed * scale
    lifted = (normed * gain).astype(jnp.bfloat16)
    pre = jnp.dot(lifted, w_in, preferred_element_type=jnp.float32)
    sigma = jax.nn.sigmoid(pre)
    hidden = (pre * sigma).astype(jnp.bfloat16)
    node_out = (nodes.astype(jnp.float32) + jnp.dot(hidden, w_out, preferred_element_type=jnp.float32)).astype(jnp.bfloat16)
    grad_hidden = jnp.dot(cotangent, w_out.T, preferred_element_type=jnp.float32)
    grad_pre = (grad_hidden * sigma * (1.0 + pre * (1.0 - sigma))).astype(jnp.bfloat16)
    grad_w_out = jnp.dot(hidden.T, cotangent, preferred_element_type=jnp.float32)
    grad_w_in = jnp.dot(lifted.T, grad_pre, preferred_element_type=jnp.float32)
    grad_lifted = jnp.dot(grad_pre, w_in.T, preferred_element_type=jnp.float32)
    grad_gain = lax.optimization_barrier(jnp.sum(grad_lifted * normed, axis=0))
    grad_normed = grad_lifted * gain
    grad_summed = (scale * (grad_normed - normed * lax.optimization_barrier(jnp.mean(grad_normed * normed, axis=-1, keepdims=True)))).astype(jnp.bfloat16)
    node_grad = (cotangent.astype(jnp.float32) + aggregate(adjacency, grad_summed)).astype(jnp.bfloat16)
    return (node_out, node_grad, grad_w_in, grad_w_out, grad_gain)
```

```python
import functools
import math

import jax
import jax.numpy as jnp
from jax import lax
from jax.experimental import pallas as pl
from jax.experimental.pallas import tpu as pltpu
from jax.sharding import PartitionSpec as P

MESH = pl.DeviceIdType.MESH
F32 = jnp.float32
BF16 = jnp.bfloat16


def dot(a, b, ca=1, cb=0):
    return lax.dot_general(a, b, (((ca,), (cb,)), ((), ())), preferred_element_type=F32)


def kernel(
    Z, PL, C, spread,
    nodes_h, adj_h, gain_ref, w_in_h, w_out_h, cot_h,
    node_out_ref, node_grad_ref, gw_ref, gg_ref,
    nodes, w_in, w_out, cot, a2, x, x2,
    part, cin, acc, pin, full, part2, cin2, acc2, pin2, full2,
    gs, lh, rh, gpart, gin, gz, gzin, gw, gg, ggp, ggz,
    loc, a_s, a_r, x_s, x_r, x2_s, x2_r,
    c_s, c_r, p_s, p_r, f_s, f_r, c2_s, c2_r, p2_s, p2_r, f2_s, f2_r,
    g_s, g_r, z_s, z_r, zg_s, zg_r, pg_s, pg_r, rg_s, rg_r,
    ggp_s, ggp_r, ggz_s, ggz_r,
):
    g = lax.axis_index("rows")
    r = lax.axis_index("rep")
    z, p = lax.div(g, PL), lax.rem(g, PL)
    ppr = Z // C
    group, D = nodes.shape
    pc = group // C
    rows_w = 2 * D // C
    w1 = rows_w // PL
    zl = lax.rem(z, ppr)
    owner = lax.div(z, ppr) == r
    sends = []

    def z_peer(d):
        return {"rows": lax.rem(z + d, Z) * PL + p}

    def p_peer(d):
        return {"rows": z * PL + lax.rem(p + d, PL)}

    def r_peer(d):
        return {"rep": lax.rem(r + d, C)}

    def rcopy(src, dst, ss, rs, dev):
        return pltpu.make_async_remote_copy(
            src_ref=src, dst_ref=dst, send_sem=ss, recv_sem=rs, device_id=dev, device_id_type=MESH
        )

    def send(src, dst, ss, rs, dev):
        c = rcopy(src, dst, ss, rs, dev)
        c.start()
        sends.append(c)

    def arrived(dst, ss, rs, dev):
        rcopy(dst, dst, ss, rs, dev).wait_recv()

    own_cols = [
        pltpu.make_async_copy(
            adj_h.at[:, pl.ds(pl.multiple_of((k * PL + p) * group, group), group)],
            a2.at[pl.ds(pl.multiple_of(p * group, group), group), pl.ds(k * group, group)],
            loc.at[4 + k],
        )
        for k in range(ppr)
    ]
    loads = [
        pltpu.make_async_copy(cot_h, cot, loc.at[0]),
        pltpu.make_async_copy(w_out_h, w_out, loc.at[1]),
        pltpu.make_async_copy(w_in_h, w_in, loc.at[2]),
        pltpu.make_async_copy(nodes_h, nodes, loc.at[3]),
    ]
    loads[3].start()
    for c in own_cols:
        c.start()
    for c in loads[:3]:
        c.start()

    barrier = pltpu.get_barrier_semaphore()
    for n, peer in ((Z, z_peer), (PL, p_peer), (C, r_peer)):
        for d in range(1, n):
            pl.semaphore_signal(barrier, inc=1, device_id=peer(d), device_id_type=MESH)
    loads[3].wait()
    pl.semaphore_wait(barrier, Z + PL + C - 3)

    def z_copies(src, buf, ss, rs):
        slot = buf.at[pl.ds(pl.multiple_of(zl * group, group), group)]
        return [rcopy(src, slot, ss.at[d - 1], rs.at[zl], z_peer(d)) for d in range(1, Z)]

    def z_start(src, buf, ss, rs):
        @pl.when(owner)
        def _():
            for c in z_copies(src, buf, ss, rs):
                c.start()
            buf[pl.ds(pl.multiple_of(zl * group, group), group)] = src[...]

    def z_wait(src, buf, ss, rs):
        for k in range(ppr):
            @pl.when(r * ppr + k != z)
            def _():
                arrived(buf.at[pl.ds(k * group, group)], ss.at[0], rs.at[k], z_peer(1))

    def z_drain(src, buf, ss, rs):
        @pl.when(owner)
        def _():
            for c in z_copies(src, buf, ss, rs):
                c.wait_send()

    z_start(nodes, x, x_s, x_r)
    for d in range(1, PL):
        q = lax.rem(p + d, PL)
        for k in range(ppr):
            send(
                adj_h.at[:, pl.ds(pl.multiple_of((k * PL + q) * group, group), group)],
                a2.at[pl.ds(pl.multiple_of(p * group, group), group), pl.ds(k * group, group)],
                a_s.at[(d - 1) * ppr + k], a_r.at[(d - 1) * ppr + k], p_peer(d),
            )

    loads[0].wait()
    loads[1].wait()
    grad_hidden = dot(cot[...], w_out[...], 1, 1)
    loads[2].wait()
    for c in own_cols:
        c.wait()
    for d in range(1, PL):
        q = lax.rem(p + PL - d, PL)
        for k in range(ppr):
            arrived(
                a2.at[pl.ds(pl.multiple_of(q * group, group), group), pl.ds(k * group, group)],
                a_s.at[(d - 1) * ppr + k], a_r.at[(d - 1) * ppr + k], p_peer(d),
            )

    def partials(buf, out, ins, ss, rs):
        for q in range(PL):
            val = dot(a2[q * group:(q + 1) * group], buf[...])
            for c in range(C):
                out[c, q] = val[c * pc:(c + 1) * pc].astype(out.dtype)
        for d in range(1, C):
            send(out.at[lax.rem(r + d, C)], ins.at[d - 1], ss.at[d - 1], rs.at[d - 1], r_peer(d))

    def combine(out, ins, ss, rs, accs, pins, pss, prs):
        for d in range(1, C):
            arrived(ins.at[d - 1], ss.at[d - 1], rs.at[d - 1], r_peer(d))
        for d in list(range(1, PL)) + [0]:
            q = lax.rem(p + d, PL)
            val = out[r, q].astype(F32)
            for e in range(C - 1):
                val = val + ins[e, q].astype(F32)
            if d == 0:
                return val
            accs[d - 1] = val.astype(accs.dtype)
            send(accs.at[d - 1], pins.at[d - 1], pss.at[d - 1], prs.at[d - 1], p_peer(d))

    def finish(val, accs, pins, pss, prs):
        for d in range(1, PL):
            arrived(pins.at[d - 1], pss.at[d - 1], prs.at[d - 1], p_peer(d))
            val = val + pins[d - 1].astype(F32)
        return val

    def piece_of(buf, c):
        return buf.at[pl.ds(pl.multiple_of(c * pc, pc), pc)]

    def share(buf, ss, rs):
        for d in range(1, C):
            send(piece_of(buf, r), piece_of(buf, r), ss.at[d - 1], rs.at[d - 1], r_peer(d))

    def shared(buf, ss, rs):
        for d in range(1, C):
            arrived(piece_of(buf, lax.rem(r + C - d, C)), ss.at[d - 1], rs.at[d - 1], r_peer(d))

    mine = pl.ds(pl.multiple_of(r * pc, pc), pc)
    z_wait(nodes, x, x_s, x_r)
    partials(x, part, cin, c_s, c_r)
    own = combine(part, cin, c_s, c_r, acc, pin, p_s, p_r)
    full[mine] = finish(own, acc, pin, p_s, p_r)
    share(full, f_s, f_r)
    shared(full, f_s, f_r)

    summed = full[...]
    gain = gain_ref[...]
    scale = lax.rsqrt(jnp.mean(summed * summed, axis=-1, keepdims=True) + 1e-05)
    normed = summed * scale
    lifted = (normed * gain).astype(BF16)
    pre = dot(lifted, w_in[...])
    sigma = jax.nn.sigmoid(pre)
    hidden = (pre * sigma).astype(BF16)
    grad_pre = (grad_hidden * sigma * (1.0 + pre * (1.0 - sigma))).astype(BF16)
    grad_lifted = dot(grad_pre, w_in[...], 1, 1)
    grad_normed = grad_lifted * gain
    gs[...] = (
        scale * (grad_normed - normed * jnp.mean(grad_normed * normed, axis=-1, keepdims=True))
    ).astype(BF16)
    z_start(gs, x2, x2_s, x2_r)

    lh[0] = lifted
    lh[1] = hidden
    rh[0] = grad_pre
    rh[1] = cot[...]
    half = C // 2
    which = lax.div(r, half)
    first = lax.rem(r, half) * rows_w
    left = lh[which, :, pl.ds(pl.multiple_of(first, rows_w), rows_w)] if half > 1 else lh[which]
    gval = dot(left, rh[which], 0, 0)
    for q in range(PL):
        gpart[q] = gval[q * w1:(q + 1) * w1].astype(BF16)
    for d in range(1, PL):
        send(gpart.at[lax.rem(p + d, PL)], gin.at[d - 1], g_s.at[d - 1], g_r.at[d - 1], p_peer(d))
    gg[...] = jnp.broadcast_to(jnp.sum(grad_lifted * normed, axis=0, keepdims=True), gg.shape)
    ggp[p] = gg[...]
    for d in range(1, PL):
        send(gg, ggp.at[p], ggp_s.at[d - 1], ggp_r.at[d - 1], p_peer(d))
    node_out_ref[...] = (nodes[...].astype(F32) + dot(hidden, w_out[...])).astype(BF16)

    z_wait(gs, x2, x2_s, x2_r)
    partials(x2, part2, cin2, c2_s, c2_r)

    gsum = gpart[p].astype(F32)
    for d in range(1, PL):
        arrived(gin.at[d - 1], g_s.at[d - 1], g_r.at[d - 1], p_peer(d))
        gsum = gsum + gin[d - 1].astype(F32)
    base = r * rows_w + p * w1
    if spread:
        wz = w1 // Z
        for k in range(Z):
            gz[k] = gsum[k * wz:(k + 1) * wz].astype(BF16)
        for d in range(1, Z):
            send(gz.at[lax.rem(z + d, Z)], gzin.at[d - 1], z_s.at[d - 1], z_r.at[d - 1], z_peer(d))
    else:
        gz[0] = gsum.astype(BF16)
        gzin[z] = gz[0]
        for d in range(1, Z):
            send(gz.at[0], gzin.at[z], z_s.at[d - 1], z_r.at[d - 1], z_peer(d))

    for d in range(1, PL):
        arrived(ggp.at[lax.rem(p + PL - d, PL)], ggp_s.at[d - 1], ggp_r.at[d - 1], p_peer(d))
    ggv = ggp[0]
    for q in range(1, PL):
        ggv = ggv + ggp[q]
    ggz[z] = ggv
    for d in range(1, Z):
        send(ggz.at[z], ggz.at[z], ggz_s.at[d - 1], ggz_r.at[d - 1], z_peer(d))

    own2 = combine(part2, cin2, c2_s, c2_r, acc2, pin2, p2_s, p2_r)

    def gw_rows(start, count):
        return gw.at[pl.ds(pl.multiple_of(start, count), count)]

    if spread:
        shard = gz[z].astype(F32)
        for d in range(1, Z):
            arrived(gzin.at[d - 1], z_s.at[d - 1], z_r.at[d - 1], z_peer(d))
            shard = shard + gzin[d - 1].astype(F32)
        here = base + z * wz
        gw[pl.ds(pl.multiple_of(here, wz), wz)] = shard.astype(BF16)
        for d in range(1, Z):
            send(gw_rows(here, wz), gw_rows(here, wz), zg_s.at[d - 1], zg_r.at[d - 1], z_peer(d))
    else:
        for d in range(1, Z):
            arrived(gzin.at[lax.rem(z + Z - d, Z)], z_s.at[d - 1], z_r.at[d - 1], z_peer(d))
        shard = gzin[0].astype(F32)
        for k in range(1, Z):
            shard = shard + gzin[k].astype(F32)
        gw[pl.ds(pl.multiple_of(base, w1), w1)] = shard.astype(BF16)

    back = finish(own2, acc2, pin2, p2_s, p2_r)
    full2[mine] = (cot[mine].astype(F32) + back).astype(BF16)
    share(full2, f2_s, f2_r)

    if spread:
        for d in range(1, Z):
            there = base + lax.rem(z + Z - d, Z) * wz
            arrived(gw_rows(there, wz), zg_s.at[d - 1], zg_r.at[d - 1], z_peer(d))
    for d in range(1, PL):
        send(gw_rows(base, w1), gw_rows(base, w1), pg_s.at[d - 1], pg_r.at[d - 1], p_peer(d))
    for d in range(PL):
        q = lax.rem(p + PL - d, PL)
        block = gw_rows(r * rows_w + q * w1, w1)
        if d > 0:
            arrived(block, pg_s.at[d - 1], pg_r.at[d - 1], p_peer(d))
        for e in range(1, C):
            i = d * (C - 1) + e - 1
            send(block, block, rg_s.at[i], rg_r.at[i], r_peer(e))

    for d in range(1, Z):
        arrived(ggz.at[lax.rem(z + Z - d, Z)], ggz_s.at[d - 1], ggz_r.at[d - 1], z_peer(d))
    ggv = ggz[0]
    for k in range(1, Z):
        ggv = ggv + ggz[k]
    gg_ref[...] = ggv
    shared(full2, f2_s, f2_r)
    node_grad_ref[...] = full2[...]
    for d in range(PL):
        q = lax.rem(p + PL - d, PL)
        for e in range(1, C):
            i = d * (C - 1) + e - 1
            there = lax.rem(r + C - e, C) * rows_w + q * w1
            arrived(gw_rows(there, w1), rg_s.at[i], rg_r.at[i], r_peer(e))
    gw_ref[...] = gw[...]
    for c in sends:
        c.wait_send()
    z_drain(nodes, x, x_s, x_r)
    z_drain(gs, x2, x2_s, x2_r)


def shards(Z, PL, C, nodes, adjacency, gain, w_in, w_out, cotangent):
    group, D = nodes.shape
    ppr = Z // C
    pc = group // C
    rows_w = 2 * D // C
    w1 = rows_w // PL
    spread = w1 % (16 * Z) == 0
    wz = w1 // Z if spread else w1
    V = pltpu.VMEM
    S = pltpu.SemaphoreType.DMA

    def pair(n):
        return [S((n,)), S((n,))]

    scratch = [
        V((group, D), BF16), V((D, D), BF16), V((D, D), BF16), V((group, D), BF16),
        V((PL * group, ppr * group), BF16), V((ppr * group, D), BF16), V((ppr * group, D), BF16),
        V((C, PL, pc, D), F32), V((C - 1, PL, pc, D), F32), V((PL - 1, pc, D), F32),
        V((PL - 1, pc, D), F32), V((group, D), F32),
        V((C, PL, pc, D), BF16), V((C - 1, PL, pc, D), BF16), V((PL - 1, pc, D), BF16),
        V((PL - 1, pc, D), BF16), V((group, D), BF16),
        V((group, D), BF16), V((2, group, D), BF16), V((2, group, D), BF16),
        V((PL, w1, D), BF16), V((PL - 1, w1, D), BF16),
        V((Z if spread else 1, wz, D), BF16), V((Z - 1 if spread else Z, wz, D), BF16),
        V((2 * D, D), BF16),
        V((8, D), F32), V((PL, 8, D), F32), V((Z, 8, D), F32),
        S((4 + ppr,)),
        *pair((PL - 1) * ppr),
        S((Z - 1,)), S((ppr,)), S((Z - 1,)), S((ppr,)),
        *pair(C - 1), *pair(PL - 1), *pair(C - 1),
        *pair(C - 1), *pair(PL - 1), *pair(C - 1),
        *pair(PL - 1), *pair(Z - 1), *pair(Z - 1), *pair(PL - 1), *pair(PL * (C - 1)),
        *pair(PL - 1), *pair(Z - 1),
    ]
    A = pl.BlockSpec(memory_space=pl.ANY)
    M = pl.BlockSpec(memory_space=pltpu.VMEM)
    node_out, node_grad, gw, gg = pl.pallas_call(
        functools.partial(kernel, Z, PL, C, spread),
        out_shape=[
            jax.ShapeDtypeStruct((group, D), BF16),
            jax.ShapeDtypeStruct((group, D), BF16),
            jax.ShapeDtypeStruct((2 * D, D), BF16),
            jax.ShapeDtypeStruct((8, D), F32),
        ],
        in_specs=[A, A, M, A, A, A],
        out_specs=[M, M, M, M],
        scratch_shapes=scratch,
        compiler_params=pltpu.CompilerParams(
            collective_id=0, has_side_effects=True, vmem_limit_bytes=40 * 1024 * 1024
        ),
    )(nodes, adjacency, gain.reshape(1, D), w_in, w_out, cotangent)
    gw = gw.astype(F32)
    return node_out, node_grad, gw[:D], gw[D:], gg[0]


def solution(mesh):
    R, C = mesh.shape["rows"], mesh.shape["rep"]
    PL = math.isqrt(R)
    return jax.shard_map(
        functools.partial(shards, R // PL, PL, C),
        mesh=mesh,
        in_specs=(P("rows", None), P("rows", "rep"), P(), P(), P(), P("rows", None)),
        out_specs=(P("rows", None), P("rows", None), P(), P(), P()),
        check_vma=False,
    )
```

```python
import functools
import math

import jax
import jax.numpy as jnp
from jax import lax
from jax.experimental import pallas as pl
from jax.experimental.pallas import tpu as pltpu
from jax.sharding import PartitionSpec as P

MESH = pl.DeviceIdType.MESH
F32 = jnp.float32
BF16 = jnp.bfloat16


def dot(a, b, ca=1, cb=0):
    return lax.dot_general(a, b, (((ca,), (cb,)), ((), ())), preferred_element_type=F32)


def kernel(
    Z, PL, C, spread,
    nodes_h, adj_h, gain_ref, w_in_h, w_out_h, cot_h,
    node_out_h, node_grad_h, gw_h, gg_h,
    nodes, w_in, w_out, cot, a2, x, x2,
    part, cin, acc, pin, full, part2, cin2, acc2, pin2, full2,
    gs, lh, rh, gpart, gin, gz, gzin, gw, gg, ggp, ggz, no_v, gg_v,
    loc, st, a_s, a_r, x_s, x_r, x2_s, x2_r,
    c_s, c_r, p_s, p_r, f_s, f_r, c2_s, c2_r, p2_s, p2_r, f2_s, f2_r,
    g_s, g_r, z_s, z_r, zg_s, zg_r, pg_s, pg_r, rg_s, rg_r,
    ggp_s, ggp_r, ggz_s, ggz_r,
):
    g = lax.axis_index("rows")
    r = lax.axis_index("rep")
    z, p = lax.div(g, PL), lax.rem(g, PL)
    ppr = Z // C
    group, D = nodes.shape
    pc = group // C
    rows_w = 2 * D // C
    w1 = rows_w // PL
    zl = lax.rem(z, ppr)
    owner = lax.div(z, ppr) == r
    sends = []
    stores = []

    def store(src, dst):
        c = pltpu.make_async_copy(src, dst, st.at[len(stores)])
        c.start()
        stores.append(c)

    def z_peer(d):
        return {"rows": lax.rem(z + d, Z) * PL + p}

    def p_peer(d):
        return {"rows": z * PL + lax.rem(p + d, PL)}

    def r_peer(d):
        return {"rep": lax.rem(r + d, C)}

    def rcopy(src, dst, ss, rs, dev):
        return pltpu.make_async_remote_copy(
            src_ref=src, dst_ref=dst, send_sem=ss, recv_sem=rs, device_id=dev, device_id_type=MESH
        )

    def send(src, dst, ss, rs, dev):
        c = rcopy(src, dst, ss, rs, dev)
        c.start()
        sends.append(c)

    def arrived(dst, ss, rs, dev):
        rcopy(dst, dst, ss, rs, dev).wait_recv()

    own_cols = [
        pltpu.make_async_copy(
            adj_h.at[:, pl.ds(pl.multiple_of((k * PL + p) * group, group), group)],
            a2.at[pl.ds(pl.multiple_of(p * group, group), group), pl.ds(k * group, group)],
            loc.at[4 + k],
        )
        for k in range(ppr)
    ]
    loads = [
        pltpu.make_async_copy(cot_h, cot, loc.at[0]),
        pltpu.make_async_copy(w_out_h, w_out, loc.at[1]),
        pltpu.make_async_copy(w_in_h, w_in, loc.at[2]),
        pltpu.make_async_copy(nodes_h, nodes, loc.at[3]),
    ]
    loads[3].start()
    for c in own_cols:
        c.start()
    for c in loads[:3]:
        c.start()

    barrier = pltpu.get_barrier_semaphore()
    for n, peer in ((Z, z_peer), (PL, p_peer), (C, r_peer)):
        for d in range(1, n):
            pl.semaphore_signal(barrier, inc=1, device_id=peer(d), device_id_type=MESH)
    loads[3].wait()
    pl.semaphore_wait(barrier, Z + PL + C - 3)

    def z_copies(src, buf, ss, rs):
        slot = buf.at[pl.ds(pl.multiple_of(zl * group, group), group)]
        return [rcopy(src, slot, ss.at[d - 1], rs.at[zl], z_peer(d)) for d in range(1, Z)]

    def z_start(src, buf, ss, rs):
        @pl.when(owner)
        def _():
            for c in z_copies(src, buf, ss, rs):
                c.start()
            buf[pl.ds(pl.multiple_of(zl * group, group), group)] = src[...]

    def z_wait(src, buf, ss, rs):
        for k in range(ppr):
            @pl.when(r * ppr + k != z)
            def _():
                arrived(buf.at[pl.ds(k * group, group)], ss.at[0], rs.at[k], z_peer(1))

    def z_drain(src, buf, ss, rs):
        @pl.when(owner)
        def _():
            for c in z_copies(src, buf, ss, rs):
                c.wait_send()

    z_start(nodes, x, x_s, x_r)
    for d in range(1, PL):
        q = lax.rem(p + d, PL)
        for k in range(ppr):
            send(
                adj_h.at[:, pl.ds(pl.multiple_of((k * PL + q) * group, group), group)],
                a2.at[pl.ds(pl.multiple_of(p * group, group), group), pl.ds(k * group, group)],
                a_s.at[(d - 1) * ppr + k], a_r.at[(d - 1) * ppr + k], p_peer(d),
            )

    loads[0].wait()
    loads[1].wait()
    grad_hidden = dot(cot[...], w_out[...], 1, 1)
    loads[2].wait()
    for c in own_cols:
        c.wait()
    for d in range(1, PL):
        q = lax.rem(p + PL - d, PL)
        for k in range(ppr):
            arrived(
                a2.at[pl.ds(pl.multiple_of(q * group, group), group), pl.ds(k * group, group)],
                a_s.at[(d - 1) * ppr + k], a_r.at[(d - 1) * ppr + k], p_peer(d),
            )

    order = list(range(1, PL)) + [0]

    def partials(buf, out, ins, ss, rs):
        for d in order:
            q = lax.rem(p + d, PL)
            val = dot(a2[pl.ds(pl.multiple_of(q * group, group), group)], buf[...])
            for c in range(C):
                out[c, d] = val[c * pc:(c + 1) * pc].astype(out.dtype)
            for e in range(1, C):
                i = d * (C - 1) + e - 1
                send(out.at[lax.rem(r + e, C), d], ins.at[e - 1, d], ss.at[i], rs.at[i], r_peer(e))

    def combine(out, ins, ss, rs, accs, pins, pss, prs):
        for d in order:
            val = out[r, d].astype(F32)
            for e in range(1, C):
                i = d * (C - 1) + e - 1
                arrived(ins.at[e - 1, d], ss.at[i], rs.at[i], r_peer(e))
                val = val + ins[e - 1, d].astype(F32)
            if d == 0:
                return val
            accs[d - 1] = val.astype(accs.dtype)
            send(accs.at[d - 1], pins.at[d - 1], pss.at[d - 1], prs.at[d - 1], p_peer(d))

    def finish(val, accs, pins, pss, prs):
        for d in range(1, PL):
            arrived(pins.at[d - 1], pss.at[d - 1], prs.at[d - 1], p_peer(d))
            val = val + pins[d - 1].astype(F32)
        return val

    def piece_of(buf, c):
        return buf.at[pl.ds(pl.multiple_of(c * pc, pc), pc)]

    def share(buf, ss, rs):
        for d in range(1, C):
            send(piece_of(buf, r), piece_of(buf, r), ss.at[d - 1], rs.at[d - 1], r_peer(d))

    def shared(buf, ss, rs):
        for d in range(1, C):
            arrived(piece_of(buf, lax.rem(r + C - d, C)), ss.at[d - 1], rs.at[d - 1], r_peer(d))

    mine = pl.ds(pl.multiple_of(r * pc, pc), pc)
    z_wait(nodes, x, x_s, x_r)
    partials(x, part, cin, c_s, c_r)
    own = combine(part, cin, c_s, c_r, acc, pin, p_s, p_r)
    full[mine] = finish(own, acc, pin, p_s, p_r)
    share(full, f_s, f_r)
    shared(full, f_s, f_r)

    summed = full[...]
    gain = gain_ref[...]
    scale = lax.rsqrt(jnp.mean(summed * summed, axis=-1, keepdims=True) + 1e-05)
    normed = summed * scale
    lifted = (normed * gain).astype(BF16)
    pre = dot(lifted, w_in[...])
    sigma = jax.nn.sigmoid(pre)
    hidden = (pre * sigma).astype(BF16)
    grad_pre = (grad_hidden * sigma * (1.0 + pre * (1.0 - sigma))).astype(BF16)
    grad_lifted = dot(grad_pre, w_in[...], 1, 1)
    grad_normed = grad_lifted * gain
    gs[...] = (
        scale * (grad_normed - normed * jnp.mean(grad_normed * normed, axis=-1, keepdims=True))
    ).astype(BF16)
    z_start(gs, x2, x2_s, x2_r)

    lh[0] = lifted
    lh[1] = hidden
    rh[0] = grad_pre
    rh[1] = cot[...]
    half = C // 2
    which = lax.div(r, half)
    first = lax.rem(r, half) * rows_w
    left = lh[which, :, pl.ds(pl.multiple_of(first, rows_w), rows_w)] if half > 1 else lh[which]
    gval = dot(left, rh[which], 0, 0)
    for q in range(PL):
        gpart[q] = gval[q * w1:(q + 1) * w1].astype(BF16)
    for d in range(1, PL):
        send(gpart.at[lax.rem(p + d, PL)], gin.at[d - 1], g_s.at[d - 1], g_r.at[d - 1], p_peer(d))
    gg[...] = jnp.broadcast_to(jnp.sum(grad_lifted * normed, axis=0, keepdims=True), gg.shape)
    ggp[p] = gg[...]
    for d in range(1, PL):
        send(gg, ggp.at[p], ggp_s.at[d - 1], ggp_r.at[d - 1], p_peer(d))
    no_v[...] = (nodes[...].astype(F32) + dot(hidden, w_out[...])).astype(BF16)
    store(no_v, node_out_h)

    z_wait(gs, x2, x2_s, x2_r)
    partials(x2, part2, cin2, c2_s, c2_r)

    gsum = gpart[p].astype(F32)
    for d in range(1, PL):
        arrived(gin.at[d - 1], g_s.at[d - 1], g_r.at[d - 1], p_peer(d))
        gsum = gsum + gin[d - 1].astype(F32)
    base = r * rows_w + p * w1
    wz = w1 // Z if spread else w1
    nz = Z if spread else 1
    if spread:
        for k in range(Z):
            gz[k] = gsum[k * wz:(k + 1) * wz].astype(BF16)
        for d in range(1, Z):
            send(gz.at[lax.rem(z + d, Z)], gzin.at[d - 1], z_s.at[d - 1], z_r.at[d - 1], z_peer(d))
    else:
        gz[0] = gsum.astype(BF16)
        gzin[z] = gz[0]
        for d in range(1, Z):
            send(gz.at[0], gzin.at[z], z_s.at[d - 1], z_r.at[d - 1], z_peer(d))

    for d in range(1, PL):
        arrived(ggp.at[lax.rem(p + PL - d, PL)], ggp_s.at[d - 1], ggp_r.at[d - 1], p_peer(d))
    ggv = ggp[0]
    for q in range(1, PL):
        ggv = ggv + ggp[q]
    ggz[z] = ggv
    for d in range(1, Z):
        send(ggz.at[z], ggz.at[z], ggz_s.at[d - 1], ggz_r.at[d - 1], z_peer(d))

    own2 = combine(part2, cin2, c2_s, c2_r, acc2, pin2, p2_s, p2_r)

    def gw_rows(start, count):
        return gw.at[pl.ds(pl.multiple_of(start, count), count)]

    if spread:
        shard = gz[z].astype(F32)
        for d in range(1, Z):
            arrived(gzin.at[d - 1], z_s.at[d - 1], z_r.at[d - 1], z_peer(d))
            shard = shard + gzin[d - 1].astype(F32)
        here = base + z * wz
        gw[pl.ds(pl.multiple_of(here, wz), wz)] = shard.astype(BF16)
        for d in range(1, Z):
            send(gw_rows(here, wz), gw_rows(here, wz), zg_s.at[d - 1], zg_r.at[d - 1], z_peer(d))
    else:
        for d in range(1, Z):
            arrived(gzin.at[lax.rem(z + Z - d, Z)], z_s.at[d - 1], z_r.at[d - 1], z_peer(d))
        shard = gzin[0].astype(F32)
        for k in range(1, Z):
            shard = shard + gzin[k].astype(F32)
        gw[pl.ds(pl.multiple_of(base, w1), w1)] = shard.astype(BF16)

    def plane_send(start, count, k):
        for d in range(1, PL):
            i = k * (PL - 1) + d - 1
            send(gw_rows(start, count), gw_rows(start, count), pg_s.at[i], pg_r.at[i], p_peer(d))

    plane_send(base + z * wz if spread else base, wz, 0)

    back = finish(own2, acc2, pin2, p2_s, p2_r)
    full2[mine] = (cot[mine].astype(F32) + back).astype(BF16)
    share(full2, f2_s, f2_r)

    for k in range(1, nz):
        there = base + lax.rem(z + Z - k, Z) * wz
        arrived(gw_rows(there, wz), zg_s.at[k - 1], zg_r.at[k - 1], z_peer(k))
        plane_send(there, wz, k)
    for d in range(PL):
        q = lax.rem(p + PL - d, PL)
        start = r * rows_w + q * w1
        if d > 0:
            for k in range(nz):
                there = start + lax.rem(z + Z - k, Z) * wz if spread else start
                i = k * (PL - 1) + d - 1
                arrived(gw_rows(there, wz), pg_s.at[i], pg_r.at[i], p_peer(d))
        block = gw_rows(start, w1)
        for e in range(1, C):
            i = d * (C - 1) + e - 1
            send(block, block, rg_s.at[i], rg_r.at[i], r_peer(e))
        store(block, gw_h.at[pl.ds(pl.multiple_of(start, w1), w1)])

    for d in range(1, Z):
        arrived(ggz.at[lax.rem(z + Z - d, Z)], ggz_s.at[d - 1], ggz_r.at[d - 1], z_peer(d))
    ggv = ggz[0]
    for k in range(1, Z):
        ggv = ggv + ggz[k]
    gg_v[...] = ggv[:1]
    store(gg_v, gg_h)
    shared(full2, f2_s, f2_r)
    store(full2, node_grad_h)
    for d in range(PL):
        q = lax.rem(p + PL - d, PL)
        for e in range(1, C):
            i = d * (C - 1) + e - 1
            there = lax.rem(r + C - e, C) * rows_w + q * w1
            arrived(gw_rows(there, w1), rg_s.at[i], rg_r.at[i], r_peer(e))
            store(gw_rows(there, w1), gw_h.at[pl.ds(pl.multiple_of(there, w1), w1)])
    for c in sends:
        c.wait_send()
    z_drain(nodes, x, x_s, x_r)
    z_drain(gs, x2, x2_s, x2_r)
    for c in stores:
        c.wait()


def closing(
    chunks, node_out, node_grad, gw, gg, o_out, o_grad, o_win, o_wout, o_gain,
    narrow, wide, pair, gain, sem_in, sem_out,
):
    D = o_win.shape[0]
    rows = 2 * D // chunks
    cuts = [pl.ds(k * rows, rows) for k in range(chunks)]
    steps = [(gw.at[c], narrow.at[c]) for c in cuts]
    steps += [(node_out, pair.at[0]), (node_grad, pair.at[1]), (gg, gain)]
    loads = [pltpu.make_async_copy(a, b, sem_in.at[i]) for i, (a, b) in enumerate(steps)]
    for c in loads:
        c.start()
    outs = []
    for k in range(chunks):
        loads[k].wait()
        wide[cuts[k]] = narrow[cuts[k]].astype(F32)
        dst = o_win if k * rows < D else o_wout
        outs.append((wide.at[cuts[k]], dst.at[pl.ds(k * rows % D, rows)]))
        pltpu.make_async_copy(*outs[k], sem_out.at[k]).start()
    outs += [(pair.at[0], o_out), (pair.at[1], o_grad), (gain, o_gain)]
    for k in range(chunks, chunks + 3):
        loads[k].wait()
        pltpu.make_async_copy(*outs[k], sem_out.at[k]).start()
    for k in range(chunks + 3):
        pltpu.make_async_copy(*outs[k], sem_out.at[k]).wait()


def shards(Z, PL, C, nodes, adjacency, gain, w_in, w_out, cotangent):
    group, D = nodes.shape
    ppr = Z // C
    pc = group // C
    rows_w = 2 * D // C
    w1 = rows_w // PL
    spread = w1 % (16 * Z) == 0
    wz = w1 // Z if spread else w1
    V = pltpu.VMEM
    S = pltpu.SemaphoreType.DMA

    def pair(n):
        return [S((n,)), S((n,))]

    scratch = [
        V((group, D), BF16), V((D, D), BF16), V((D, D), BF16), V((group, D), BF16),
        V((PL * group, ppr * group), BF16), V((ppr * group, D), BF16), V((ppr * group, D), BF16),
        V((C, PL, pc, D), F32), V((C - 1, PL, pc, D), F32), V((PL - 1, pc, D), F32),
        V((PL - 1, pc, D), F32), V((group, D), F32),
        V((C, PL, pc, D), BF16), V((C - 1, PL, pc, D), BF16), V((PL - 1, pc, D), BF16),
        V((PL - 1, pc, D), BF16), V((group, D), BF16),
        V((group, D), BF16), V((2, group, D), BF16), V((2, group, D), BF16),
        V((PL, w1, D), BF16), V((PL - 1, w1, D), BF16),
        V((Z if spread else 1, wz, D), BF16), V((Z - 1 if spread else Z, wz, D), BF16),
        V((2 * D, D), BF16),
        V((8, D), F32), V((PL, 8, D), F32), V((Z, 8, D), F32), V((group, D), BF16), V((1, D), F32),
        S((4 + ppr,)), S((3 + PL * C,)),
        *pair((PL - 1) * ppr),
        S((Z - 1,)), S((ppr,)), S((Z - 1,)), S((ppr,)),
        *pair(PL * (C - 1)), *pair(PL - 1), *pair(C - 1),
        *pair(PL * (C - 1)), *pair(PL - 1), *pair(C - 1),
        *pair(PL - 1), *pair(Z - 1), *pair(Z - 1), *pair((PL - 1) * (w1 // wz)), *pair(PL * (C - 1)),
        *pair(PL - 1), *pair(Z - 1),
    ]
    H = pl.BlockSpec(memory_space=pltpu.HBM)
    M = pl.BlockSpec(memory_space=pltpu.VMEM)
    parts = pl.pallas_call(
        functools.partial(kernel, Z, PL, C, spread),
        out_shape=[
            jax.ShapeDtypeStruct((group, D), BF16),
            jax.ShapeDtypeStruct((group, D), BF16),
            jax.ShapeDtypeStruct((2 * D, D), BF16),
            jax.ShapeDtypeStruct((1, D), F32),
        ],
        in_specs=[H, H, M, H, H, H],
        out_specs=[H, H, H, H],
        scratch_shapes=scratch,
        compiler_params=pltpu.CompilerParams(
            collective_id=0, has_side_effects=True, vmem_limit_bytes=60 * 1024 * 1024
        ),
    )(nodes, adjacency, gain.reshape(1, D), w_in, w_out, cotangent)
    chunks = 8
    node_out, node_grad, g_in, g_out, gg = pl.pallas_call(
        functools.partial(closing, chunks),
        out_shape=[
            jax.ShapeDtypeStruct((group, D), BF16),
            jax.ShapeDtypeStruct((group, D), BF16),
            jax.ShapeDtypeStruct((D, D), F32),
            jax.ShapeDtypeStruct((D, D), F32),
            jax.ShapeDtypeStruct((1, D), F32),
        ],
        in_specs=[H, H, H, H],
        out_specs=[H, H, H, H, H],
        scratch_shapes=[
            V((2 * D, D), BF16), V((2 * D, D), F32), V((2, group, D), BF16), V((1, D), F32),
            S((chunks + 3,)), S((chunks + 3,)),
        ],
        compiler_params=pltpu.CompilerParams(vmem_limit_bytes=60 * 1024 * 1024),
    )(*parts)
    return node_out, node_grad, g_in, g_out, gg.reshape(D)


def solution(mesh):
    R, C = mesh.shape["rows"], mesh.shape["rep"]
    PL = math.isqrt(R)
    return jax.shard_map(
        functools.partial(shards, R // PL, PL, C),
        mesh=mesh,
        in_specs=(P("rows", None), P("rows", "rep"), P(), P(), P(), P("rows", None)),
        out_specs=(P("rows", None), P("rows", None), P(), P(), P()),
        check_vma=False,
    )
```

```python
import functools
import math

import jax
import jax.numpy as jnp
from jax import lax
from jax.experimental import pallas as pl
from jax.experimental.pallas import tpu as pltpu
from jax.sharding import PartitionSpec as P

MESH = pl.DeviceIdType.MESH
F32 = jnp.float32
BF16 = jnp.bfloat16


def dot(a, b, ca=1, cb=0):
    return lax.dot_general(a, b, (((ca,), (cb,)), ((), ())), preferred_element_type=F32)


def kernel(
    Z, PL, C, T, spread,
    nodes_h, adj_h, gain_ref, w_in_h, w_out_h, cot_h,
    node_out_h, node_grad_h, gw_h, gg_h,
    nodes, w_in, w_out, cot, a2, x, x2,
    part, cin, acc, pin, full, part2, cin2, acc2, pin2, full2,
    gs, lh, rh, gpart, gin, gz, gzin, gw, gg, ggp, ggz, no_v, gg_v,
    loc, st, a_s, a_r, x_s, x_r, x2_s, x2_r,
    c_s, c_r, p_s, p_r, f_s, f_r, c2_s, c2_r, p2_s, p2_r, f2_s, f2_r,
    g_s, g_r, z_s, z_r, zg_s, zg_r, pg_s, pg_r, rg_s, rg_r,
    ggp_s, ggp_r, ggz_s, ggz_r,
):
    g = lax.axis_index("rows")
    r = lax.axis_index("rep")
    z, p = lax.div(g, PL), lax.rem(g, PL)
    ppr = Z // C
    group, D = nodes.shape
    pc = group // C
    rows_w = 2 * D // C // T
    w1 = rows_w // PL
    wz = w1 // Z if spread else w1
    zl = lax.rem(z, ppr)
    owner = lax.div(z, ppr) == r
    sends = []
    stores = []

    def store(src, dst):
        c = pltpu.make_async_copy(src, dst, st.at[len(stores)])
        c.start()
        stores.append(c)

    def z_peer(d):
        return {"rows": lax.rem(z + d, Z) * PL + p}

    def p_peer(d):
        return {"rows": z * PL + lax.rem(p + d, PL)}

    def r_peer(d):
        return {"rep": lax.rem(r + d, C)}

    def rcopy(src, dst, ss, rs, dev):
        return pltpu.make_async_remote_copy(
            src_ref=src, dst_ref=dst, send_sem=ss, recv_sem=rs, device_id=dev, device_id_type=MESH
        )

    def send(src, dst, ss, rs, dev):
        c = rcopy(src, dst, ss, rs, dev)
        c.start()
        sends.append(c)

    def arrived(dst, ss, rs, dev):
        rcopy(dst, dst, ss, rs, dev).wait_recv()

    own_cols = [
        pltpu.make_async_copy(
            adj_h.at[:, pl.ds(pl.multiple_of((k * PL + p) * group, group), group)],
            a2.at[pl.ds(pl.multiple_of(p * group, group), group), pl.ds(k * group, group)],
            loc.at[4 + k],
        )
        for k in range(ppr)
    ]
    loads = [
        pltpu.make_async_copy(cot_h, cot, loc.at[0]),
        pltpu.make_async_copy(w_out_h, w_out, loc.at[1]),
        pltpu.make_async_copy(w_in_h, w_in, loc.at[2]),
        pltpu.make_async_copy(nodes_h, nodes, loc.at[3]),
    ]
    loads[3].start()
    for c in own_cols:
        c.start()
    for c in loads[:3]:
        c.start()

    barrier = pltpu.get_barrier_semaphore()
    for n, peer in ((Z, z_peer), (PL, p_peer), (C, r_peer)):
        for d in range(1, n):
            pl.semaphore_signal(barrier, inc=1, device_id=peer(d), device_id_type=MESH)
    loads[3].wait()
    pl.semaphore_wait(barrier, Z + PL + C - 3)

    def z_copies(src, buf, ss, rs):
        slot = buf.at[pl.ds(pl.multiple_of(zl * group, group), group)]
        return [rcopy(src, slot, ss.at[d - 1], rs.at[zl], z_peer(d)) for d in range(1, Z)]

    def z_start(src, buf, ss, rs):
        @pl.when(owner)
        def _():
            for c in z_copies(src, buf, ss, rs):
                c.start()
            buf[pl.ds(pl.multiple_of(zl * group, group), group)] = src[...]

    def z_wait(src, buf, ss, rs):
        for k in range(ppr):
            @pl.when(r * ppr + k != z)
            def _():
                arrived(buf.at[pl.ds(k * group, group)], ss.at[0], rs.at[k], z_peer(1))

    def z_drain(src, buf, ss, rs):
        @pl.when(owner)
        def _():
            for c in z_copies(src, buf, ss, rs):
                c.wait_send()

    z_start(nodes, x, x_s, x_r)
    for d in range(1, PL):
        q = lax.rem(p + d, PL)
        for k in range(ppr):
            send(
                adj_h.at[:, pl.ds(pl.multiple_of((k * PL + q) * group, group), group)],
                a2.at[pl.ds(pl.multiple_of(p * group, group), group), pl.ds(k * group, group)],
                a_s.at[(d - 1) * ppr + k], a_r.at[(d - 1) * ppr + k], p_peer(d),
            )

    loads[0].wait()
    loads[1].wait()
    grad_hidden = dot(cot[...], w_out[...], 1, 1)
    loads[2].wait()
    for c in own_cols:
        c.wait()
    for d in range(1, PL):
        q = lax.rem(p + PL - d, PL)
        for k in range(ppr):
            arrived(
                a2.at[pl.ds(pl.multiple_of(q * group, group), group), pl.ds(k * group, group)],
                a_s.at[(d - 1) * ppr + k], a_r.at[(d - 1) * ppr + k], p_peer(d),
            )

    order = list(range(1, PL)) + [0]

    def partials(buf, out, ins, ss, rs):
        for d in order:
            q = lax.rem(p + d, PL)
            val = dot(a2[pl.ds(pl.multiple_of(q * group, group), group)], buf[...])
            for c in range(C):
                out[c, d] = val[c * pc:(c + 1) * pc].astype(out.dtype)
            for e in range(1, C):
                i = d * (C - 1) + e - 1
                send(out.at[lax.rem(r + e, C), d], ins.at[e - 1, d], ss.at[i], rs.at[i], r_peer(e))

    def combine(out, ins, ss, rs, accs, pins, pss, prs):
        for d in order:
            val = out[r, d].astype(F32)
            for e in range(1, C):
                i = d * (C - 1) + e - 1
                arrived(ins.at[e - 1, d], ss.at[i], rs.at[i], r_peer(e))
                val = val + ins[e - 1, d].astype(F32)
            if d == 0:
                return val
            accs[d - 1] = val.astype(accs.dtype)
            send(accs.at[d - 1], pins.at[d - 1], pss.at[d - 1], prs.at[d - 1], p_peer(d))

    def finish(val, accs, pins, pss, prs):
        for d in range(1, PL):
            arrived(pins.at[d - 1], pss.at[d - 1], prs.at[d - 1], p_peer(d))
            val = val + pins[d - 1].astype(F32)
        return val

    def piece_of(buf, c):
        return buf.at[pl.ds(pl.multiple_of(c * pc, pc), pc)]

    def share(buf, ss, rs):
        for d in range(1, C):
            send(piece_of(buf, r), piece_of(buf, r), ss.at[d - 1], rs.at[d - 1], r_peer(d))

    def shared(buf, ss, rs):
        for d in range(1, C):
            arrived(piece_of(buf, lax.rem(r + C - d, C)), ss.at[d - 1], rs.at[d - 1], r_peer(d))

    mine = pl.ds(pl.multiple_of(r * pc, pc), pc)
    z_wait(nodes, x, x_s, x_r)
    partials(x, part, cin, c_s, c_r)
    own = combine(part, cin, c_s, c_r, acc, pin, p_s, p_r)
    full[mine] = finish(own, acc, pin, p_s, p_r)
    share(full, f_s, f_r)
    shared(full, f_s, f_r)

    summed = full[...]
    gain = gain_ref[...]
    scale = lax.rsqrt(jnp.mean(summed * summed, axis=-1, keepdims=True) + 1e-05)
    normed = summed * scale
    lifted = (normed * gain).astype(BF16)
    pre = dot(lifted, w_in[...])
    sigma = jax.nn.sigmoid(pre)
    hidden = (pre * sigma).astype(BF16)

    def first_row(t, rep):
        if T == 1:
            return rep * rows_w
        return (1 - t) * D + rep * rows_w

    def weights_start(t, left, right):
        gval = dot(left, right, 0, 0)
        for q in range(PL):
            gpart[t, q] = gval[q * w1:(q + 1) * w1].astype(BF16)
        for d in range(1, PL):
            i = t * (PL - 1) + d - 1
            send(gpart.at[t, lax.rem(p + d, PL)], gin.at[i], g_s.at[i], g_r.at[i], p_peer(d))

    def columns(ref):
        return ref[:, pl.ds(pl.multiple_of(r * rows_w, rows_w), rows_w)]

    lh[1] = hidden
    if T == 2:
        weights_start(0, columns(lh.at[1]), cot[...])
    grad_pre = (grad_hidden * sigma * (1.0 + pre * (1.0 - sigma))).astype(BF16)
    grad_lifted = dot(grad_pre, w_in[...], 1, 1)
    grad_normed = grad_lifted * gain
    gs[...] = (
        scale * (grad_normed - normed * jnp.mean(grad_normed * normed, axis=-1, keepdims=True))
    ).astype(BF16)
    z_start(gs, x2, x2_s, x2_r)

    lh[0] = lifted
    if T == 2:
        weights_start(1, columns(lh.at[0]), grad_pre)
    else:
        rh[0] = grad_pre
        rh[1] = cot[...]
        half = C // 2
        which = lax.div(r, half)
        here = pl.multiple_of(lax.rem(r, half) * rows_w, rows_w)
        weights_start(0, lh[which, :, pl.ds(here, rows_w)], rh[which])
    gg[...] = jnp.broadcast_to(jnp.sum(grad_lifted * normed, axis=0, keepdims=True), gg.shape)
    ggp[p] = gg[...]
    for d in range(1, PL):
        send(gg, ggp.at[p], ggp_s.at[d - 1], ggp_r.at[d - 1], p_peer(d))
    no_v[...] = (nodes[...].astype(F32) + dot(hidden, w_out[...])).astype(BF16)
    store(no_v, node_out_h)

    def gw_rows(start, count):
        return gw.at[pl.ds(pl.multiple_of(start, count), count)]

    def scatter_z(t):
        gsum = gpart[t, p].astype(F32)
        for d in range(1, PL):
            i = t * (PL - 1) + d - 1
            arrived(gin.at[i], g_s.at[i], g_r.at[i], p_peer(d))
            gsum = gsum + gin[i].astype(F32)
        if spread:
            for k in range(Z):
                gz[t, k] = gsum[k * wz:(k + 1) * wz].astype(BF16)
        else:
            gz[t, 0] = gsum.astype(BF16)
            gzin[t, z] = gz[t, 0]
        for d in range(1, Z):
            i = t * (Z - 1) + d - 1
            src = gz.at[t, lax.rem(z + d, Z)] if spread else gz.at[t, 0]
            dst = gzin.at[t, d - 1] if spread else gzin.at[t, z]
            send(src, dst, z_s.at[i], z_r.at[i], z_peer(d))

    def gather_z(t):
        base = first_row(t, r) + p * w1
        shard = gz[t, z].astype(F32) if spread else None
        for d in range(1, Z):
            i = t * (Z - 1) + d - 1
            slot = gzin.at[t, d - 1] if spread else gzin.at[t, lax.rem(z + Z - d, Z)]
            arrived(slot, z_s.at[i], z_r.at[i], z_peer(d))
            if spread:
                shard = shard + gzin[t, d - 1].astype(F32)
        if not spread:
            shard = gzin[t, 0].astype(F32)
            for k in range(1, Z):
                shard = shard + gzin[t, k].astype(F32)
            gw[pl.ds(pl.multiple_of(base, w1), w1)] = shard.astype(BF16)
            return
        here = base + z * wz
        gw[pl.ds(pl.multiple_of(here, wz), wz)] = shard.astype(BF16)
        for d in range(1, Z):
            i = t * (Z - 1) + d - 1
            send(gw_rows(here, wz), gw_rows(here, wz), zg_s.at[i], zg_r.at[i], z_peer(d))

    def gather_plane(t):
        base = first_row(t, r) + p * w1
        if spread:
            for d in range(1, Z):
                i = t * (Z - 1) + d - 1
                there = base + lax.rem(z + Z - d, Z) * wz
                arrived(gw_rows(there, wz), zg_s.at[i], zg_r.at[i], z_peer(d))
        for d in range(1, PL):
            i = t * (PL - 1) + d - 1
            send(gw_rows(base, w1), gw_rows(base, w1), pg_s.at[i], pg_r.at[i], p_peer(d))

    def keep(start):
        store(gw_rows(start, w1), gw_h.at[pl.ds(pl.multiple_of(start, w1), w1)])

    def gather_rep(t):
        for d in range(PL):
            start = first_row(t, r) + lax.rem(p + PL - d, PL) * w1
            block = gw_rows(start, w1)
            if d > 0:
                i = t * (PL - 1) + d - 1
                arrived(block, pg_s.at[i], pg_r.at[i], p_peer(d))
            for e in range(1, C):
                i = (t * PL + d) * (C - 1) + e - 1
                send(block, block, rg_s.at[i], rg_r.at[i], r_peer(e))
            keep(start)

    def gather_end(t):
        for d in range(PL):
            for e in range(1, C):
                i = (t * PL + d) * (C - 1) + e - 1
                start = first_row(t, lax.rem(r + C - e, C)) + lax.rem(p + PL - d, PL) * w1
                arrived(gw_rows(start, w1), rg_s.at[i], rg_r.at[i], r_peer(e))
                keep(start)

    last = T - 1
    for t in range(T):
        scatter_z(t)
    if T == 2:
        gather_z(0)
    z_wait(gs, x2, x2_s, x2_r)
    partials(x2, part2, cin2, c2_s, c2_r)
    gather_z(last)
    own2 = combine(part2, cin2, c2_s, c2_r, acc2, pin2, p2_s, p2_r)
    for t in range(T):
        gather_plane(t)

    for d in range(1, PL):
        arrived(ggp.at[lax.rem(p + PL - d, PL)], ggp_s.at[d - 1], ggp_r.at[d - 1], p_peer(d))
    ggv = ggp[0]
    for q in range(1, PL):
        ggv = ggv + ggp[q]
    ggz[z] = ggv
    for d in range(1, Z):
        send(ggz.at[z], ggz.at[z], ggz_s.at[d - 1], ggz_r.at[d - 1], z_peer(d))

    back = finish(own2, acc2, pin2, p2_s, p2_r)
    full2[mine] = (cot[mine].astype(F32) + back).astype(BF16)
    share(full2, f2_s, f2_r)
    gather_rep(0)
    shared(full2, f2_s, f2_r)
    store(full2, node_grad_h)
    if T == 2:
        gather_rep(1)
    for d in range(1, Z):
        arrived(ggz.at[lax.rem(z + Z - d, Z)], ggz_s.at[d - 1], ggz_r.at[d - 1], z_peer(d))
    ggv = ggz[0]
    for k in range(1, Z):
        ggv = ggv + ggz[k]
    gg_v[...] = ggv[:1]
    store(gg_v, gg_h)
    for t in range(T):
        gather_end(t)
    for c in sends:
        c.wait_send()
    z_drain(nodes, x, x_s, x_r)
    z_drain(gs, x2, x2_s, x2_r)
    for c in stores:
        c.wait()


def closing(
    chunks, node_out, node_grad, gw, gg, o_out, o_grad, o_win, o_wout, o_gain,
    narrow, wide, pair, gain, sem_in, sem_out,
):
    D = o_win.shape[0]
    rows = 2 * D // chunks
    cuts = [pl.ds(k * rows, rows) for k in range(chunks)]
    steps = [(gw.at[c], narrow.at[c]) for c in cuts]
    steps += [(node_out, pair.at[0]), (node_grad, pair.at[1]), (gg, gain)]
    loads = [pltpu.make_async_copy(a, b, sem_in.at[i]) for i, (a, b) in enumerate(steps)]
    for c in loads:
        c.start()
    outs = []
    for k in range(chunks):
        loads[k].wait()
        wide[cuts[k]] = narrow[cuts[k]].astype(F32)
        dst = o_win if k * rows < D else o_wout
        outs.append((wide.at[cuts[k]], dst.at[pl.ds(k * rows % D, rows)]))
        pltpu.make_async_copy(*outs[k], sem_out.at[k]).start()
    outs += [(pair.at[0], o_out), (pair.at[1], o_grad), (gain, o_gain)]
    for k in range(chunks, chunks + 3):
        loads[k].wait()
        pltpu.make_async_copy(*outs[k], sem_out.at[k]).start()
    for k in range(chunks + 3):
        pltpu.make_async_copy(*outs[k], sem_out.at[k]).wait()


def shards(Z, PL, C, nodes, adjacency, gain, w_in, w_out, cotangent):
    group, D = nodes.shape
    ppr = Z // C
    pc = group // C
    T = 2 if D // C // PL % (16 * Z) == 0 else 1
    w1 = 2 * D // C // T // PL
    spread = w1 % (16 * Z) == 0
    wz = w1 // Z if spread else w1
    V = pltpu.VMEM
    S = pltpu.SemaphoreType.DMA

    def pair(n):
        return [S((n,)), S((n,))]

    scratch = [
        V((group, D), BF16), V((D, D), BF16), V((D, D), BF16), V((group, D), BF16),
        V((PL * group, ppr * group), BF16), V((ppr * group, D), BF16), V((ppr * group, D), BF16),
        V((C, PL, pc, D), F32), V((C - 1, PL, pc, D), F32), V((PL - 1, pc, D), F32),
        V((PL - 1, pc, D), F32), V((group, D), F32),
        V((C, PL, pc, D), BF16), V((C - 1, PL, pc, D), BF16), V((PL - 1, pc, D), BF16),
        V((PL - 1, pc, D), BF16), V((group, D), BF16),
        V((group, D), BF16), V((2, group, D), BF16), V((2, group, D), BF16),
        V((T, PL, w1, D), BF16), V((T * (PL - 1), w1, D), BF16),
        V((T, Z if spread else 1, wz, D), BF16), V((T, Z - 1 if spread else Z, wz, D), BF16),
        V((2 * D, D), BF16),
        V((8, D), F32), V((PL, 8, D), F32), V((Z, 8, D), F32), V((group, D), BF16), V((1, D), F32),
        S((4 + ppr,)), S((3 + T * PL * C,)),
        *pair((PL - 1) * ppr),
        S((Z - 1,)), S((ppr,)), S((Z - 1,)), S((ppr,)),
        *pair(PL * (C - 1)), *pair(PL - 1), *pair(C - 1),
        *pair(PL * (C - 1)), *pair(PL - 1), *pair(C - 1),
        *pair(T * (PL - 1)), *pair(T * (Z - 1)), *pair(T * (Z - 1)), *pair(T * (PL - 1)),
        *pair(T * PL * (C - 1)),
        *pair(PL - 1), *pair(Z - 1),
    ]
    H = pl.BlockSpec(memory_space=pltpu.HBM)
    M = pl.BlockSpec(memory_space=pltpu.VMEM)
    parts = pl.pallas_call(
        functools.partial(kernel, Z, PL, C, T, spread),
        out_shape=[
            jax.ShapeDtypeStruct((group, D), BF16),
            jax.ShapeDtypeStruct((group, D), BF16),
            jax.ShapeDtypeStruct((2 * D, D), BF16),
            jax.ShapeDtypeStruct((1, D), F32),
        ],
        in_specs=[H, H, M, H, H, H],
        out_specs=[H, H, H, H],
        scratch_shapes=scratch,
        compiler_params=pltpu.CompilerParams(
            collective_id=0, has_side_effects=True, vmem_limit_bytes=60 * 1024 * 1024
        ),
    )(nodes, adjacency, gain.reshape(1, D), w_in, w_out, cotangent)
    chunks = 8
    node_out, node_grad, g_in, g_out, gg = pl.pallas_call(
        functools.partial(closing, chunks),
        out_shape=[
            jax.ShapeDtypeStruct((group, D), BF16),
            jax.ShapeDtypeStruct((group, D), BF16),
            jax.ShapeDtypeStruct((D, D), F32),
            jax.ShapeDtypeStruct((D, D), F32),
            jax.ShapeDtypeStruct((1, D), F32),
        ],
        in_specs=[H, H, H, H],
        out_specs=[H, H, H, H, H],
        scratch_shapes=[
            V((2 * D, D), BF16), V((2 * D, D), F32), V((2, group, D), BF16), V((1, D), F32),
            S((chunks + 3,)), S((chunks + 3,)),
        ],
        compiler_params=pltpu.CompilerParams(vmem_limit_bytes=60 * 1024 * 1024),
    )(*parts)
    return node_out, node_grad, g_in, g_out, gg.reshape(D)


def solution(mesh):
    R, C = mesh.shape["rows"], mesh.shape["rep"]
    PL = math.isqrt(R)
    return jax.shard_map(
        functools.partial(shards, R // PL, PL, C),
        mesh=mesh,
        in_specs=(P("rows", None), P("rows", "rep"), P(), P(), P(), P("rows", None)),
        out_specs=(P("rows", None), P("rows", None), P(), P(), P()),
        check_vma=False,
    )
```

```python
import functools
import math

import jax
import jax.numpy as jnp
from jax import lax
from jax.experimental import pallas as pl
from jax.experimental.pallas import tpu as pltpu
from jax.sharding import PartitionSpec as P

MESH = pl.DeviceIdType.MESH
F32 = jnp.float32
BF16 = jnp.bfloat16


def dot(a, b, ca=1, cb=0):
    return lax.dot_general(a, b, (((ca,), (cb,)), ((), ())), preferred_element_type=F32)


def kernel(
    Z, PL, C, T, spread, feat,
    nodes_h, adj_h, gain_ref, w_in_h, w_out_h, cot_h,
    node_out_h, node_grad_h, gw_h, gg_h,
    nodes, w_in, w_out, cot, a2, x, x2,
    part, cin, acc, pin, full, part2, cin2, acc2, pin2, full2,
    gs, lh, rh, gpart, gin, gz, gzin, gw, gg, ggp, ggz, no_v, gg_v,
    loc, st, a_s, a_r, ar_s, ar_r, x_s, x_r, x2_s, x2_r,
    c_s, c_r, p_s, p_r, f_s, f_r, c2_s, c2_r, p2_s, p2_r, f2_s, f2_r,
    g_s, g_r, z_s, z_r, zg_s, zg_r, pg_s, pg_r, rg_s, rg_r,
    ggp_s, ggp_r, ggz_s, ggz_r,
):
    g = lax.axis_index("rows")
    r = lax.axis_index("rep")
    z, p = lax.div(g, PL), lax.rem(g, PL)
    ppr = Z // C
    group, D = nodes.shape
    pc = group // C
    rows_w = 2 * D // C // T
    w1 = rows_w // PL
    wz = w1 // Z if spread else w1
    zl = lax.rem(z, ppr)
    owner = lax.div(z, ppr) == r
    lead = r * ppr if feat else 0
    Dc = D // C
    my_cols = pl.ds(pl.multiple_of(r * Dc, Dc), Dc)
    sends = []
    stores = []

    def store(src, dst):
        c = pltpu.make_async_copy(src, dst, st.at[len(stores)])
        c.start()
        stores.append(c)

    def z_peer(d):
        return {"rows": lax.rem(z + d, Z) * PL + p}

    def p_peer(d):
        return {"rows": z * PL + lax.rem(p + d, PL)}

    def r_peer(d):
        return {"rep": lax.rem(r + d, C)}

    def rcopy(src, dst, ss, rs, dev):
        return pltpu.make_async_remote_copy(
            src_ref=src, dst_ref=dst, send_sem=ss, recv_sem=rs, device_id=dev, device_id_type=MESH
        )

    def send(src, dst, ss, rs, dev):
        c = rcopy(src, dst, ss, rs, dev)
        c.start()
        sends.append(c)

    def arrived(dst, ss, rs, dev):
        rcopy(dst, dst, ss, rs, dev).wait_recv()

    def cols_of(k):
        return pl.ds(pl.multiple_of((lead + k) * group, group), group)

    own_cols = [
        pltpu.make_async_copy(
            adj_h.at[:, pl.ds(pl.multiple_of((k * PL + p) * group, group), group)],
            a2.at[pl.ds(pl.multiple_of(p * group, group), group), cols_of(k)],
            loc.at[4 + k],
        )
        for k in range(ppr)
    ]
    loads = [
        pltpu.make_async_copy(cot_h, cot, loc.at[0]),
        pltpu.make_async_copy(w_out_h, w_out, loc.at[1]),
        pltpu.make_async_copy(w_in_h, w_in, loc.at[2]),
        pltpu.make_async_copy(nodes_h, nodes, loc.at[3]),
    ]
    loads[3].start()
    for c in own_cols:
        c.start()
    for c in loads[:3]:
        c.start()

    barrier = pltpu.get_barrier_semaphore()
    for n, peer in ((Z, z_peer), (PL, p_peer), (C, r_peer)):
        for d in range(1, n):
            pl.semaphore_signal(barrier, inc=1, device_id=peer(d), device_id_type=MESH)
    loads[3].wait()
    pl.semaphore_wait(barrier, Z + PL + C - 3)

    def z_rows(k):
        return pl.ds(pl.multiple_of(k * group, group), group)

    def z_copies(src, buf, ss, rs):
        if feat:
            slot = buf.at[z_rows(z)]
            return [
                rcopy(src.at[:, my_cols], slot, ss.at[d - 1], rs.at[d - 1], z_peer(d))
                for d in range(1, Z)
            ]
        slot = buf.at[pl.ds(pl.multiple_of(zl * group, group), group)]
        return [rcopy(src, slot, ss.at[d - 1], rs.at[zl], z_peer(d)) for d in range(1, Z)]

    def z_start(src, buf, ss, rs):
        if feat:
            for c in z_copies(src, buf, ss, rs):
                c.start()
            buf[z_rows(z)] = src[:, my_cols]
            return

        @pl.when(owner)
        def _():
            for c in z_copies(src, buf, ss, rs):
                c.start()
            buf[pl.ds(pl.multiple_of(zl * group, group), group)] = src[...]

    def z_wait(src, buf, ss, rs):
        if feat:
            for d in range(1, Z):
                slot = buf.at[z_rows(lax.rem(z + Z - d, Z))]
                arrived(slot, ss.at[d - 1], rs.at[d - 1], z_peer(d))
            return
        for k in range(ppr):
            @pl.when(r * ppr + k != z)
            def _():
                arrived(buf.at[pl.ds(k * group, group)], ss.at[0], rs.at[k], z_peer(1))

    def z_drain(src, buf, ss, rs):
        if feat:
            for c in z_copies(src, buf, ss, rs):
                c.wait_send()
            return

        @pl.when(owner)
        def _():
            for c in z_copies(src, buf, ss, rs):
                c.wait_send()

    z_start(nodes, x, x_s, x_r)
    for d in range(1, PL):
        q = lax.rem(p + d, PL)
        for k in range(ppr):
            send(
                adj_h.at[:, pl.ds(pl.multiple_of((k * PL + q) * group, group), group)],
                a2.at[pl.ds(pl.multiple_of(p * group, group), group), cols_of(k)],
                a_s.at[(d - 1) * ppr + k], a_r.at[(d - 1) * ppr + k], p_peer(d),
            )

    loads[0].wait()
    loads[1].wait()
    grad_hidden = dot(cot[...], w_out[...], 1, 1)
    loads[2].wait()
    for c in own_cols:
        c.wait()

    def halves(d, e):
        q = lax.rem(p + PL - d, PL)
        there = pl.multiple_of(lax.rem(r + C - e, C) * ppr * group, ppr * group)
        return a2.at[pl.ds(pl.multiple_of(q * group, group), group), pl.ds(there, ppr * group)]

    def forward(d):
        for e in range(1, C):
            i = d * (C - 1) + e - 1
            send(halves(d, 0), halves(d, 0), ar_s.at[i], ar_r.at[i], r_peer(e))

    if feat:
        forward(0)
    for d in range(1, PL):
        q = lax.rem(p + PL - d, PL)
        for k in range(ppr):
            arrived(
                a2.at[pl.ds(pl.multiple_of(q * group, group), group), cols_of(k)],
                a_s.at[(d - 1) * ppr + k], a_r.at[(d - 1) * ppr + k], p_peer(d),
            )
        if feat:
            forward(d)
    if feat:
        for d in range(PL):
            for e in range(1, C):
                i = d * (C - 1) + e - 1
                arrived(halves(d, e), ar_s.at[i], ar_r.at[i], r_peer(e))

    order = list(range(1, PL)) + [0]

    def partials(buf, out, ins, ss, rs):
        for d in order:
            q = lax.rem(p + d, PL)
            val = dot(a2[pl.ds(pl.multiple_of(q * group, group), group)], buf[...])
            for c in range(C):
                out[c, d] = val[c * pc:(c + 1) * pc].astype(out.dtype)
            for e in range(1, C):
                i = d * (C - 1) + e - 1
                send(out.at[lax.rem(r + e, C), d], ins.at[e - 1, d], ss.at[i], rs.at[i], r_peer(e))

    def combine(out, ins, ss, rs, accs, pins, pss, prs):
        for d in order:
            val = out[r, d].astype(F32)
            for e in range(1, C):
                i = d * (C - 1) + e - 1
                arrived(ins.at[e - 1, d], ss.at[i], rs.at[i], r_peer(e))
                val = val + ins[e - 1, d].astype(F32)
            if d == 0:
                return val
            accs[d - 1] = val.astype(accs.dtype)
            send(accs.at[d - 1], pins.at[d - 1], pss.at[d - 1], prs.at[d - 1], p_peer(d))

    def aggregate(buf, out, ins, ss, rs, accs, pins, pss, prs):
        if not feat:
            partials(buf, out, ins, ss, rs)
            return combine(out, ins, ss, rs, accs, pins, pss, prs)
        for d in order:
            q = lax.rem(p + d, PL)
            val = dot(a2[pl.ds(pl.multiple_of(q * group, group), group)], buf[...])
            if d == 0:
                return val
            accs[d - 1] = val.astype(accs.dtype)
            send(accs.at[d - 1], pins.at[d - 1], pss.at[d - 1], prs.at[d - 1], p_peer(d))

    def finish(val, accs, pins, pss, prs):
        for d in range(1, PL):
            arrived(pins.at[d - 1], pss.at[d - 1], prs.at[d - 1], p_peer(d))
            val = val + pins[d - 1].astype(F32)
        return val

    def piece_of(buf, c):
        if feat:
            return buf.at[:, pl.ds(pl.multiple_of(c * Dc, Dc), Dc)]
        return buf.at[pl.ds(pl.multiple_of(c * pc, pc), pc)]

    def share(buf, ss, rs):
        for d in range(1, C):
            send(piece_of(buf, r), piece_of(buf, r), ss.at[d - 1], rs.at[d - 1], r_peer(d))

    def shared(buf, ss, rs):
        for d in range(1, C):
            arrived(piece_of(buf, lax.rem(r + C - d, C)), ss.at[d - 1], rs.at[d - 1], r_peer(d))

    if feat:
        mine = (slice(None), my_cols)
    else:
        mine = pl.ds(pl.multiple_of(r * pc, pc), pc)
    z_wait(nodes, x, x_s, x_r)
    own = aggregate(x, part, cin, c_s, c_r, acc, pin, p_s, p_r)
    full[mine] = finish(own, acc, pin, p_s, p_r)
    share(full, f_s, f_r)
    shared(full, f_s, f_r)

    summed = full[...]
    gain = gain_ref[...]
    scale = lax.rsqrt(jnp.mean(summed * summed, axis=-1, keepdims=True) + 1e-05)
    normed = summed * scale
    lifted = (normed * gain).astype(BF16)
    pre = dot(lifted, w_in[...])
    sigma = jax.nn.sigmoid(pre)
    hidden = (pre * sigma).astype(BF16)

    def first_row(t, rep):
        if T == 1:
            return rep * rows_w
        return (1 - t) * D + rep * rows_w

    def weights_start(t, left, right):
        gval = dot(left, right, 0, 0)
        for q in range(PL):
            gpart[t, q] = gval[q * w1:(q + 1) * w1].astype(BF16)
        for d in range(1, PL):
            i = t * (PL - 1) + d - 1
            send(gpart.at[t, lax.rem(p + d, PL)], gin.at[i], g_s.at[i], g_r.at[i], p_peer(d))

    def columns(ref):
        return ref[:, pl.ds(pl.multiple_of(r * rows_w, rows_w), rows_w)]

    lh[1] = hidden
    if T == 2:
        weights_start(0, columns(lh.at[1]), cot[...])
    grad_pre = (grad_hidden * sigma * (1.0 + pre * (1.0 - sigma))).astype(BF16)
    grad_lifted = dot(grad_pre, w_in[...], 1, 1)
    grad_normed = grad_lifted * gain
    gs[...] = (
        scale * (grad_normed - normed * jnp.mean(grad_normed * normed, axis=-1, keepdims=True))
    ).astype(BF16)
    z_start(gs, x2, x2_s, x2_r)

    lh[0] = lifted
    if T == 2:
        weights_start(1, columns(lh.at[0]), grad_pre)
    else:
        rh[0] = grad_pre
        rh[1] = cot[...]
        half = C // 2
        which = lax.div(r, half)
        here = pl.multiple_of(lax.rem(r, half) * rows_w, rows_w)
        weights_start(0, lh[which, :, pl.ds(here, rows_w)], rh[which])
    gg[...] = jnp.broadcast_to(jnp.sum(grad_lifted * normed, axis=0, keepdims=True), gg.shape)
    ggp[p] = gg[...]
    for d in range(1, PL):
        send(gg, ggp.at[p], ggp_s.at[d - 1], ggp_r.at[d - 1], p_peer(d))
    no_v[...] = (nodes[...].astype(F32) + dot(hidden, w_out[...])).astype(BF16)
    store(no_v, node_out_h)

    def gw_rows(start, count):
        return gw.at[pl.ds(pl.multiple_of(start, count), count)]

    def scatter_z(t):
        gsum = gpart[t, p].astype(F32)
        for d in range(1, PL):
            i = t * (PL - 1) + d - 1
            arrived(gin.at[i], g_s.at[i], g_r.at[i], p_peer(d))
            gsum = gsum + gin[i].astype(F32)
        if spread:
            for k in range(Z):
                gz[t, k] = gsum[k * wz:(k + 1) * wz].astype(BF16)
        else:
            gz[t, 0] = gsum.astype(BF16)
            gzin[t, z] = gz[t, 0]
        for d in range(1, Z):
            i = t * (Z - 1) + d - 1
            src = gz.at[t, lax.rem(z + d, Z)] if spread else gz.at[t, 0]
            dst = gzin.at[t, d - 1] if spread else gzin.at[t, z]
            send(src, dst, z_s.at[i], z_r.at[i], z_peer(d))

    def gather_z(t):
        base = first_row(t, r) + p * w1
        shard = gz[t, z].astype(F32) if spread else None
        for d in range(1, Z):
            i = t * (Z - 1) + d - 1
            slot = gzin.at[t, d - 1] if spread else gzin.at[t, lax.rem(z + Z - d, Z)]
            arrived(slot, z_s.at[i], z_r.at[i], z_peer(d))
            if spread:
                shard = shard + gzin[t, d - 1].astype(F32)
        if not spread:
            shard = gzin[t, 0].astype(F32)
            for k in range(1, Z):
                shard = shard + gzin[t, k].astype(F32)
            gw[pl.ds(pl.multiple_of(base, w1), w1)] = shard.astype(BF16)
            return
        here = base + z * wz
        gw[pl.ds(pl.multiple_of(here, wz), wz)] = shard.astype(BF16)
        for d in range(1, Z):
            i = t * (Z - 1) + d - 1
            send(gw_rows(here, wz), gw_rows(here, wz), zg_s.at[i], zg_r.at[i], z_peer(d))

    def gather_plane(t):
        base = first_row(t, r) + p * w1
        if spread:
            for d in range(1, Z):
                i = t * (Z - 1) + d - 1
                there = base + lax.rem(z + Z - d, Z) * wz
                arrived(gw_rows(there, wz), zg_s.at[i], zg_r.at[i], z_peer(d))
        for d in range(1, PL):
            i = t * (PL - 1) + d - 1
            send(gw_rows(base, w1), gw_rows(base, w1), pg_s.at[i], pg_r.at[i], p_peer(d))

    def keep(start):
        store(gw_rows(start, w1), gw_h.at[pl.ds(pl.multiple_of(start, w1), w1)])

    def gather_rep(t):
        for d in range(PL):
            start = first_row(t, r) + lax.rem(p + PL - d, PL) * w1
            block = gw_rows(start, w1)
            if d > 0:
                i = t * (PL - 1) + d - 1
                arrived(block, pg_s.at[i], pg_r.at[i], p_peer(d))
            for e in range(1, C):
                i = (t * PL + d) * (C - 1) + e - 1
                send(block, block, rg_s.at[i], rg_r.at[i], r_peer(e))
            keep(start)

    def gather_end(t):
        for d in range(PL):
            for e in range(1, C):
                i = (t * PL + d) * (C - 1) + e - 1
                start = first_row(t, lax.rem(r + C - e, C)) + lax.rem(p + PL - d, PL) * w1
                arrived(gw_rows(start, w1), rg_s.at[i], rg_r.at[i], r_peer(e))
                keep(start)

    last = T - 1
    for t in range(T):
        scatter_z(t)
    if T == 2:
        gather_z(0)
    z_wait(gs, x2, x2_s, x2_r)
    own2 = aggregate(x2, part2, cin2, c2_s, c2_r, acc2, pin2, p2_s, p2_r)
    gather_z(last)
    for t in range(T):
        gather_plane(t)

    for d in range(1, PL):
        arrived(ggp.at[lax.rem(p + PL - d, PL)], ggp_s.at[d - 1], ggp_r.at[d - 1], p_peer(d))
    ggv = ggp[0]
    for q in range(1, PL):
        ggv = ggv + ggp[q]
    ggz[z] = ggv
    for d in range(1, Z):
        send(ggz.at[z], ggz.at[z], ggz_s.at[d - 1], ggz_r.at[d - 1], z_peer(d))

    back = finish(own2, acc2, pin2, p2_s, p2_r)
    full2[mine] = (cot[mine].astype(F32) + back).astype(BF16)
    share(full2, f2_s, f2_r)
    gather_rep(0)
    shared(full2, f2_s, f2_r)
    store(full2, node_grad_h)
    if T == 2:
        gather_rep(1)
    for d in range(1, Z):
        arrived(ggz.at[lax.rem(z + Z - d, Z)], ggz_s.at[d - 1], ggz_r.at[d - 1], z_peer(d))
    ggv = ggz[0]
    for k in range(1, Z):
        ggv = ggv + ggz[k]
    gg_v[...] = ggv[:1]
    store(gg_v, gg_h)
    for t in range(T):
        gather_end(t)
    for c in sends:
        c.wait_send()
    z_drain(nodes, x, x_s, x_r)
    z_drain(gs, x2, x2_s, x2_r)
    for c in stores:
        c.wait()


def closing(
    chunks, node_out, node_grad, gw, gg, o_out, o_grad, o_win, o_wout, o_gain,
    narrow, wide, pair, gain, sem_in, sem_out,
):
    D = o_win.shape[0]
    rows = 2 * D // chunks
    cuts = [pl.ds(k * rows, rows) for k in range(chunks)]
    steps = [(gw.at[c], narrow.at[c]) for c in cuts]
    steps += [(node_out, pair.at[0]), (node_grad, pair.at[1]), (gg, gain)]
    loads = [pltpu.make_async_copy(a, b, sem_in.at[i]) for i, (a, b) in enumerate(steps)]
    for c in loads:
        c.start()
    outs = []
    for k in range(chunks):
        loads[k].wait()
        wide[cuts[k]] = narrow[cuts[k]].astype(F32)
        dst = o_win if k * rows < D else o_wout
        outs.append((wide.at[cuts[k]], dst.at[pl.ds(k * rows % D, rows)]))
        pltpu.make_async_copy(*outs[k], sem_out.at[k]).start()
    outs += [(pair.at[0], o_out), (pair.at[1], o_grad), (gain, o_gain)]
    for k in range(chunks, chunks + 3):
        loads[k].wait()
        pltpu.make_async_copy(*outs[k], sem_out.at[k]).start()
    for k in range(chunks + 3):
        pltpu.make_async_copy(*outs[k], sem_out.at[k]).wait()


def shards(Z, PL, C, nodes, adjacency, gain, w_in, w_out, cotangent):
    group, D = nodes.shape
    ppr = Z // C
    pc = group // C
    feat = D // C % 128 == 0
    T = 2 if D // C // PL % (16 * Z) == 0 else 1
    w1 = 2 * D // C // T // PL
    spread = w1 % (16 * Z) == 0
    wz = w1 // Z if spread else w1
    if feat:
        field, piece = (Z * group, D // C), (PL - 1, group, D // C)
        split = split_in = (8, 128)
    else:
        field, piece = (ppr * group, D), (PL - 1, pc, D)
        split, split_in = (C, PL, pc, D), (C - 1, PL, pc, D)
    V = pltpu.VMEM
    S = pltpu.SemaphoreType.DMA

    def pair(n):
        return [S((n,)), S((n,))]

    scratch = [
        V((group, D), BF16), V((D, D), BF16), V((D, D), BF16), V((group, D), BF16),
        *([V((PL * group, Z * group), BF16)] if feat else [V((PL * group, ppr * group), BF16)]),
        V(field, BF16), V(field, BF16),
        V(split, F32), V(split_in, F32), V(piece, F32), V(piece, F32), V((group, D), F32),
        V(split, BF16), V(split_in, BF16), V(piece, BF16), V(piece, BF16), V((group, D), BF16),
        V((group, D), BF16), V((2, group, D), BF16), V((2, group, D), BF16),
        V((T, PL, w1, D), BF16), V((T * (PL - 1), w1, D), BF16),
        V((T, Z if spread else 1, wz, D), BF16), V((T, Z - 1 if spread else Z, wz, D), BF16),
        V((2 * D, D), BF16),
        V((8, D), F32), V((PL, 8, D), F32), V((Z, 8, D), F32), V((group, D), BF16), V((1, D), F32),
        S((4 + ppr,)), S((3 + T * PL * C,)),
        *pair((PL - 1) * ppr), *pair(PL * (C - 1)),
        S((Z - 1,)), S((Z - 1,)), S((Z - 1,)), S((Z - 1,)),
        *pair(PL * (C - 1)), *pair(PL - 1), *pair(C - 1),
        *pair(PL * (C - 1)), *pair(PL - 1), *pair(C - 1),
        *pair(T * (PL - 1)), *pair(T * (Z - 1)), *pair(T * (Z - 1)), *pair(T * (PL - 1)),
        *pair(T * PL * (C - 1)),
        *pair(PL - 1), *pair(Z - 1),
    ]
    H = pl.BlockSpec(memory_space=pltpu.HBM)
    M = pl.BlockSpec(memory_space=pltpu.VMEM)
    parts = pl.pallas_call(
        functools.partial(kernel, Z, PL, C, T, spread, feat),
        out_shape=[
            jax.ShapeDtypeStruct((group, D), BF16),
            jax.ShapeDtypeStruct((group, D), BF16),
            jax.ShapeDtypeStruct((2 * D, D), BF16),
            jax.ShapeDtypeStruct((1, D), F32),
        ],
        in_specs=[H, H, M, H, H, H],
        out_specs=[H, H, H, H],
        scratch_shapes=scratch,
        compiler_params=pltpu.CompilerParams(
            collective_id=0, has_side_effects=True, vmem_limit_bytes=60 * 1024 * 1024
        ),
    )(nodes, adjacency, gain.reshape(1, D), w_in, w_out, cotangent)
    chunks = 8
    node_out, node_grad, g_in, g_out, gg = pl.pallas_call(
        functools.partial(closing, chunks),
        out_shape=[
            jax.ShapeDtypeStruct((group, D), BF16),
            jax.ShapeDtypeStruct((group, D), BF16),
            jax.ShapeDtypeStruct((D, D), F32),
            jax.ShapeDtypeStruct((D, D), F32),
            jax.ShapeDtypeStruct((1, D), F32),
        ],
        in_specs=[H, H, H, H],
        out_specs=[H, H, H, H, H],
        scratch_shapes=[
            V((2 * D, D), BF16), V((2 * D, D), F32), V((2, group, D), BF16), V((1, D), F32),
            S((chunks + 3,)), S((chunks + 3,)),
        ],
        compiler_params=pltpu.CompilerParams(vmem_limit_bytes=60 * 1024 * 1024),
    )(*parts)
    return node_out, node_grad, g_in, g_out, gg.reshape(D)


def solution(mesh):
    R, C = mesh.shape["rows"], mesh.shape["rep"]
    PL = math.isqrt(R)
    return jax.shard_map(
        functools.partial(shards, R // PL, PL, C),
        mesh=mesh,
        in_specs=(P("rows", None), P("rows", "rep"), P(), P(), P(), P("rows", None)),
        out_specs=(P("rows", None), P("rows", None), P(), P(), P()),
        check_vma=False,
    )
```

```python
import functools
import math

import jax
import jax.numpy as jnp
from jax import lax
from jax.experimental import pallas as pl
from jax.experimental.pallas import tpu as pltpu
from jax.sharding import PartitionSpec as P

MESH = pl.DeviceIdType.MESH
F32 = jnp.float32
BF16 = jnp.bfloat16


def dot(a, b, ca=1, cb=0):
    return lax.dot_general(a, b, (((ca,), (cb,)), ((), ())), preferred_element_type=F32)


def kernel(
    Z, PL, C, T, spread, feat, gath,
    nodes_h, adj_h, gain_ref, w_in_h, w_out_h, cot_h,
    node_out_h, node_grad_h, gw_h, gg_h,
    nodes, w_in, w_out, cot, a2, x, x2,
    part, cin, acc, pin, full, part2, cin2, acc2, pin2, full2,
    gs, lh, rh, gpart, gin, gz, gzin, gw, gg, ggp, ggz, no_v, gg_v, lall, rall,
    loc, st, a_s, a_r, ar_s, ar_r, x_s, x_r, x2_s, x2_r,
    c_s, c_r, p_s, p_r, f_s, f_r, c2_s, c2_r, p2_s, p2_r, f2_s, f2_r,
    g_s, g_r, z_s, z_r, zg_s, zg_r, pg_s, pg_r, rg_s, rg_r,
    ggp_s, ggp_r, ggz_s, ggz_r, l_s, l_r, ra_s, ra_r,
):
    g = lax.axis_index("rows")
    r = lax.axis_index("rep")
    z, p = lax.div(g, PL), lax.rem(g, PL)
    ppr = Z // C
    group, D = nodes.shape
    pc = group // C
    rows_w = 2 * D // C // T
    w1 = rows_w // PL
    wz = w1 // Z if spread else w1
    zl = lax.rem(z, ppr)
    owner = lax.div(z, ppr) == r
    lead = r * ppr if feat else 0
    Dc = D // C
    my_cols = pl.ds(pl.multiple_of(r * Dc, Dc), Dc)
    sends = []
    stores = []

    def store(src, dst):
        c = pltpu.make_async_copy(src, dst, st.at[len(stores)])
        c.start()
        stores.append(c)

    def z_peer(d):
        return {"rows": lax.rem(z + d, Z) * PL + p}

    def p_peer(d):
        return {"rows": z * PL + lax.rem(p + d, PL)}

    def r_peer(d):
        return {"rep": lax.rem(r + d, C)}

    def rcopy(src, dst, ss, rs, dev):
        return pltpu.make_async_remote_copy(
            src_ref=src, dst_ref=dst, send_sem=ss, recv_sem=rs, device_id=dev, device_id_type=MESH
        )

    def send(src, dst, ss, rs, dev):
        c = rcopy(src, dst, ss, rs, dev)
        c.start()
        sends.append(c)

    def arrived(dst, ss, rs, dev):
        rcopy(dst, dst, ss, rs, dev).wait_recv()

    def cols_of(k):
        return pl.ds(pl.multiple_of((lead + k) * group, group), group)

    own_cols = [
        pltpu.make_async_copy(
            adj_h.at[:, pl.ds(pl.multiple_of((k * PL + p) * group, group), group)],
            a2.at[pl.ds(pl.multiple_of(p * group, group), group), cols_of(k)],
            loc.at[4 + k],
        )
        for k in range(ppr)
    ]
    loads = [
        pltpu.make_async_copy(cot_h, cot, loc.at[0]),
        pltpu.make_async_copy(w_out_h, w_out, loc.at[1]),
        pltpu.make_async_copy(w_in_h, w_in, loc.at[2]),
        pltpu.make_async_copy(nodes_h, nodes, loc.at[3]),
    ]
    loads[3].start()
    for c in own_cols:
        c.start()
    for c in loads[:3]:
        c.start()

    barrier = pltpu.get_barrier_semaphore()
    for n, peer in ((Z, z_peer), (PL, p_peer), (C, r_peer)):
        for d in range(1, n):
            pl.semaphore_signal(barrier, inc=1, device_id=peer(d), device_id_type=MESH)
    loads[3].wait()
    pl.semaphore_wait(barrier, Z + PL + C - 3)

    def z_rows(k):
        return pl.ds(pl.multiple_of(k * group, group), group)

    def z_copies(src, buf, ss, rs):
        if feat:
            slot = buf.at[z_rows(z)]
            return [
                rcopy(src.at[:, my_cols], slot, ss.at[d - 1], rs.at[d - 1], z_peer(d))
                for d in range(1, Z)
            ]
        slot = buf.at[pl.ds(pl.multiple_of(zl * group, group), group)]
        return [rcopy(src, slot, ss.at[d - 1], rs.at[zl], z_peer(d)) for d in range(1, Z)]

    def z_start(src, buf, ss, rs):
        if feat:
            for c in z_copies(src, buf, ss, rs):
                c.start()
            buf[z_rows(z)] = src[:, my_cols]
            return

        @pl.when(owner)
        def _():
            for c in z_copies(src, buf, ss, rs):
                c.start()
            buf[pl.ds(pl.multiple_of(zl * group, group), group)] = src[...]

    def z_wait(src, buf, ss, rs):
        if feat:
            for d in range(1, Z):
                slot = buf.at[z_rows(lax.rem(z + Z - d, Z))]
                arrived(slot, ss.at[d - 1], rs.at[d - 1], z_peer(d))
            return
        for k in range(ppr):
            @pl.when(r * ppr + k != z)
            def _():
                arrived(buf.at[pl.ds(k * group, group)], ss.at[0], rs.at[k], z_peer(1))

    def z_drain(src, buf, ss, rs):
        if feat:
            for c in z_copies(src, buf, ss, rs):
                c.wait_send()
            return

        @pl.when(owner)
        def _():
            for c in z_copies(src, buf, ss, rs):
                c.wait_send()

    z_start(nodes, x, x_s, x_r)
    for d in range(1, PL):
        q = lax.rem(p + d, PL)
        for k in range(ppr):
            send(
                adj_h.at[:, pl.ds(pl.multiple_of((k * PL + q) * group, group), group)],
                a2.at[pl.ds(pl.multiple_of(p * group, group), group), cols_of(k)],
                a_s.at[(d - 1) * ppr + k], a_r.at[(d - 1) * ppr + k], p_peer(d),
            )

    def plane_copies(srcs, dst, ss, rs):
        slot = dst.at[z_rows(p)]
        return [rcopy(srcs(d), slot, ss.at[d - 1], rs.at[d - 1], p_peer(d)) for d in range(1, PL)]

    def left_copies(k):
        def cut(d):
            q = lax.rem(p + d, PL)
            return lh.at[k, :, pl.ds(pl.multiple_of(q * w1, w1), w1)]

        return plane_copies(cut, lall, l_s, l_r)

    def right_copies(src):
        return plane_copies(lambda d: src, rall, ra_s, ra_r)

    def begin(copies, core):
        @pl.when(r == core)
        def _():
            for c in copies():
                c.start()

    def end(copies, core):
        @pl.when(r == core)
        def _():
            for c in copies():
                c.wait_send()

    if gath:
        begin(lambda: right_copies(cot_h), 1)
    loads[0].wait()
    loads[1].wait()
    grad_hidden = dot(cot[...], w_out[...], 1, 1)
    loads[2].wait()
    for c in own_cols:
        c.wait()

    def halves(d, e):
        q = lax.rem(p + PL - d, PL)
        there = pl.multiple_of(lax.rem(r + C - e, C) * ppr * group, ppr * group)
        return a2.at[pl.ds(pl.multiple_of(q * group, group), group), pl.ds(there, ppr * group)]

    def forward(d):
        for e in range(1, C):
            i = d * (C - 1) + e - 1
            send(halves(d, 0), halves(d, 0), ar_s.at[i], ar_r.at[i], r_peer(e))

    if feat:
        forward(0)
    for d in range(1, PL):
        q = lax.rem(p + PL - d, PL)
        for k in range(ppr):
            arrived(
                a2.at[pl.ds(pl.multiple_of(q * group, group), group), cols_of(k)],
                a_s.at[(d - 1) * ppr + k], a_r.at[(d - 1) * ppr + k], p_peer(d),
            )
        if feat:
            forward(d)
    if feat:
        for d in range(PL):
            for e in range(1, C):
                i = d * (C - 1) + e - 1
                arrived(halves(d, e), ar_s.at[i], ar_r.at[i], r_peer(e))

    order = list(range(1, PL)) + [0]

    def partials(buf, out, ins, ss, rs):
        for d in order:
            q = lax.rem(p + d, PL)
            val = dot(a2[pl.ds(pl.multiple_of(q * group, group), group)], buf[...])
            for c in range(C):
                out[c, d] = val[c * pc:(c + 1) * pc].astype(out.dtype)
            for e in range(1, C):
                i = d * (C - 1) + e - 1
                send(out.at[lax.rem(r + e, C), d], ins.at[e - 1, d], ss.at[i], rs.at[i], r_peer(e))

    def combine(out, ins, ss, rs, accs, pins, pss, prs):
        for d in order:
            val = out[r, d].astype(F32)
            for e in range(1, C):
                i = d * (C - 1) + e - 1
                arrived(ins.at[e - 1, d], ss.at[i], rs.at[i], r_peer(e))
                val = val + ins[e - 1, d].astype(F32)
            if d == 0:
                return val
            accs[d - 1] = val.astype(accs.dtype)
            send(accs.at[d - 1], pins.at[d - 1], pss.at[d - 1], prs.at[d - 1], p_peer(d))

    def aggregate(buf, out, ins, ss, rs, accs, pins, pss, prs):
        if not feat:
            partials(buf, out, ins, ss, rs)
            return combine(out, ins, ss, rs, accs, pins, pss, prs)
        for d in order:
            q = lax.rem(p + d, PL)
            val = dot(a2[pl.ds(pl.multiple_of(q * group, group), group)], buf[...])
            if d == 0:
                return val
            accs[d - 1] = val.astype(accs.dtype)
            send(accs.at[d - 1], pins.at[d - 1], pss.at[d - 1], prs.at[d - 1], p_peer(d))

    def finish(val, accs, pins, pss, prs):
        for d in range(1, PL):
            arrived(pins.at[d - 1], pss.at[d - 1], prs.at[d - 1], p_peer(d))
            val = val + pins[d - 1].astype(F32)
        return val

    def piece_of(buf, c):
        if feat:
            return buf.at[:, pl.ds(pl.multiple_of(c * Dc, Dc), Dc)]
        return buf.at[pl.ds(pl.multiple_of(c * pc, pc), pc)]

    def share(buf, ss, rs):
        for d in range(1, C):
            send(piece_of(buf, r), piece_of(buf, r), ss.at[d - 1], rs.at[d - 1], r_peer(d))

    def shared(buf, ss, rs):
        for d in range(1, C):
            arrived(piece_of(buf, lax.rem(r + C - d, C)), ss.at[d - 1], rs.at[d - 1], r_peer(d))

    if feat:
        mine = (slice(None), my_cols)
    else:
        mine = pl.ds(pl.multiple_of(r * pc, pc), pc)
    z_wait(nodes, x, x_s, x_r)
    own = aggregate(x, part, cin, c_s, c_r, acc, pin, p_s, p_r)
    full[mine] = finish(own, acc, pin, p_s, p_r)
    share(full, f_s, f_r)
    shared(full, f_s, f_r)

    summed = full[...]
    gain = gain_ref[...]
    scale = lax.rsqrt(jnp.mean(summed * summed, axis=-1, keepdims=True) + 1e-05)
    normed = summed * scale
    lifted = (normed * gain).astype(BF16)
    lh[0] = lifted
    if gath:
        begin(lambda: left_copies(0), 0)
    pre = dot(lifted, w_in[...])
    sigma = jax.nn.sigmoid(pre)
    hidden = (pre * sigma).astype(BF16)

    def first_row(t, rep):
        if T == 1:
            return rep * rows_w
        return (1 - t) * D + rep * rows_w

    def weights_start(t, left, right):
        gval = dot(left, right, 0, 0)
        for q in range(PL):
            gpart[t, q] = gval[q * w1:(q + 1) * w1].astype(BF16)
        for d in range(1, PL):
            i = t * (PL - 1) + d - 1
            send(gpart.at[t, lax.rem(p + d, PL)], gin.at[i], g_s.at[i], g_r.at[i], p_peer(d))

    def columns(ref):
        return ref[:, pl.ds(pl.multiple_of(r * rows_w, rows_w), rows_w)]

    lh[1] = hidden
    if gath:
        begin(lambda: left_copies(1), 1)
    elif T == 2:
        weights_start(0, columns(lh.at[1]), cot[...])
    grad_pre = (grad_hidden * sigma * (1.0 + pre * (1.0 - sigma))).astype(BF16)
    rh[0] = grad_pre
    rh[1] = cot[...]
    if gath:
        begin(lambda: right_copies(rh.at[0]), 0)
    grad_lifted = dot(grad_pre, w_in[...], 1, 1)
    grad_normed = grad_lifted * gain
    gs[...] = (
        scale * (grad_normed - normed * jnp.mean(grad_normed * normed, axis=-1, keepdims=True))
    ).astype(BF16)
    z_start(gs, x2, x2_s, x2_r)

    if gath:
        lall[z_rows(p)] = lh[r, :, pl.ds(pl.multiple_of(p * w1, w1), w1)]
        rall[z_rows(p)] = rh[r]
    elif T == 2:
        weights_start(1, columns(lh.at[0]), grad_pre)
    else:
        half = C // 2
        which = lax.div(r, half)
        here = pl.multiple_of(lax.rem(r, half) * rows_w, rows_w)
        weights_start(0, lh[which, :, pl.ds(here, rows_w)], rh[which])
    gg[...] = jnp.broadcast_to(jnp.sum(grad_lifted * normed, axis=0, keepdims=True), gg.shape)
    ggp[p] = gg[...]
    for d in range(1, PL):
        send(gg, ggp.at[p], ggp_s.at[d - 1], ggp_r.at[d - 1], p_peer(d))
    no_v[...] = (nodes[...].astype(F32) + dot(hidden, w_out[...])).astype(BF16)
    store(no_v, node_out_h)

    def gw_rows(start, count):
        return gw.at[pl.ds(pl.multiple_of(start, count), count)]

    def scatter_z(t):
        if gath:
            for d in range(1, PL):
                slot = z_rows(lax.rem(p + PL - d, PL))
                arrived(lall.at[slot], l_s.at[d - 1], l_r.at[d - 1], p_peer(d))
                arrived(rall.at[slot], ra_s.at[d - 1], ra_r.at[d - 1], p_peer(d))
            gsum = dot(lall[...], rall[...], 0, 0)
        else:
            gsum = gpart[t, p].astype(F32)
            for d in range(1, PL):
                i = t * (PL - 1) + d - 1
                arrived(gin.at[i], g_s.at[i], g_r.at[i], p_peer(d))
                gsum = gsum + gin[i].astype(F32)
        if spread:
            for k in range(Z):
                gz[t, k] = gsum[k * wz:(k + 1) * wz].astype(BF16)
        else:
            gz[t, 0] = gsum.astype(BF16)
            gzin[t, z] = gz[t, 0]
        for d in range(1, Z):
            i = t * (Z - 1) + d - 1
            src = gz.at[t, lax.rem(z + d, Z)] if spread else gz.at[t, 0]
            dst = gzin.at[t, d - 1] if spread else gzin.at[t, z]
            send(src, dst, z_s.at[i], z_r.at[i], z_peer(d))

    def gather_z(t):
        base = first_row(t, r) + p * w1
        shard = gz[t, z].astype(F32) if spread else None
        for d in range(1, Z):
            i = t * (Z - 1) + d - 1
            slot = gzin.at[t, d - 1] if spread else gzin.at[t, lax.rem(z + Z - d, Z)]
            arrived(slot, z_s.at[i], z_r.at[i], z_peer(d))
            if spread:
                shard = shard + gzin[t, d - 1].astype(F32)
        if not spread:
            shard = gzin[t, 0].astype(F32)
            for k in range(1, Z):
                shard = shard + gzin[t, k].astype(F32)
            gw[pl.ds(pl.multiple_of(base, w1), w1)] = shard.astype(BF16)
            return
        here = base + z * wz
        gw[pl.ds(pl.multiple_of(here, wz), wz)] = shard.astype(BF16)
        for c in zg_copies(t):
            c.start()

    def zg_copies(t):
        if not spread:
            return []
        here = gw_rows(first_row(t, r) + p * w1 + z * wz, wz)
        first = t * (Z - 1) - 1
        return [rcopy(here, here, zg_s.at[first + d], zg_r.at[first + d], z_peer(d)) for d in range(1, Z)]

    def pg_copies(t):
        here = gw_rows(first_row(t, r) + p * w1, w1)
        first = t * (PL - 1) - 1
        return [rcopy(here, here, pg_s.at[first + d], pg_r.at[first + d], p_peer(d)) for d in range(1, PL)]

    def gather_plane(t):
        base = first_row(t, r) + p * w1
        if spread:
            for d in range(1, Z):
                i = t * (Z - 1) + d - 1
                there = base + lax.rem(z + Z - d, Z) * wz
                arrived(gw_rows(there, wz), zg_s.at[i], zg_r.at[i], z_peer(d))
        for c in pg_copies(t):
            c.start()

    def keep(start):
        store(gw_rows(start, w1), gw_h.at[pl.ds(pl.multiple_of(start, w1), w1)])

    def gather_rep(t):
        for d in range(PL):
            start = first_row(t, r) + lax.rem(p + PL - d, PL) * w1
            block = gw_rows(start, w1)
            if d > 0:
                i = t * (PL - 1) + d - 1
                arrived(block, pg_s.at[i], pg_r.at[i], p_peer(d))
            for e in range(1, C):
                i = (t * PL + d) * (C - 1) + e - 1
                send(block, block, rg_s.at[i], rg_r.at[i], r_peer(e))
            keep(start)

    def gather_end(t):
        for d in range(PL):
            for e in range(1, C):
                i = (t * PL + d) * (C - 1) + e - 1
                start = first_row(t, lax.rem(r + C - e, C)) + lax.rem(p + PL - d, PL) * w1
                arrived(gw_rows(start, w1), rg_s.at[i], rg_r.at[i], r_peer(e))
                keep(start)

    last = T - 1
    for t in range(T):
        scatter_z(t)
    if gath:
        @pl.when(r == 1)
        def _():
            gather_z(0)
    elif T == 2:
        gather_z(0)
    z_wait(gs, x2, x2_s, x2_r)
    own2 = aggregate(x2, part2, cin2, c2_s, c2_r, acc2, pin2, p2_s, p2_r)
    if gath:
        @pl.when(r == 1)
        def _():
            gather_plane(0)

        @pl.when(r == 0)
        def _():
            gather_z(0)
            gather_plane(0)
    else:
        gather_z(last)
        for t in range(T):
            gather_plane(t)

    for d in range(1, PL):
        arrived(ggp.at[lax.rem(p + PL - d, PL)], ggp_s.at[d - 1], ggp_r.at[d - 1], p_peer(d))
    ggv = ggp[0]
    for q in range(1, PL):
        ggv = ggv + ggp[q]
    ggz[z] = ggv
    for d in range(1, Z):
        send(ggz.at[z], ggz.at[z], ggz_s.at[d - 1], ggz_r.at[d - 1], z_peer(d))

    back = finish(own2, acc2, pin2, p2_s, p2_r)
    full2[mine] = (cot[mine].astype(F32) + back).astype(BF16)
    share(full2, f2_s, f2_r)
    gather_rep(0)
    shared(full2, f2_s, f2_r)
    store(full2, node_grad_h)
    if T == 2:
        gather_rep(1)
    for d in range(1, Z):
        arrived(ggz.at[lax.rem(z + Z - d, Z)], ggz_s.at[d - 1], ggz_r.at[d - 1], z_peer(d))
    ggv = ggz[0]
    for k in range(1, Z):
        ggv = ggv + ggz[k]
    gg_v[...] = ggv[:1]
    store(gg_v, gg_h)
    for t in range(T):
        gather_end(t)
    for c in sends:
        c.wait_send()
    for t in range(T):
        for c in zg_copies(t) + pg_copies(t):
            c.wait_send()
    if gath:
        end(lambda: left_copies(0) + right_copies(rh.at[0]), 0)
        end(lambda: left_copies(1) + right_copies(cot_h), 1)
    z_drain(nodes, x, x_s, x_r)
    z_drain(gs, x2, x2_s, x2_r)
    for c in stores:
        c.wait()


def closing(
    chunks, node_out, node_grad, gw, gg, o_out, o_grad, o_win, o_wout, o_gain,
    narrow, wide, pair, gain, sem_in, sem_out,
):
    D = o_win.shape[0]
    rows = 2 * D // chunks
    cuts = [pl.ds(k * rows, rows) for k in range(chunks)]
    steps = [(gw.at[c], narrow.at[c]) for c in cuts]
    steps += [(node_out, pair.at[0]), (node_grad, pair.at[1]), (gg, gain)]
    loads = [pltpu.make_async_copy(a, b, sem_in.at[i]) for i, (a, b) in enumerate(steps)]
    for c in loads:
        c.start()
    outs = []
    for k in range(chunks):
        loads[k].wait()
        wide[cuts[k]] = narrow[cuts[k]].astype(F32)
        dst = o_win if k * rows < D else o_wout
        outs.append((wide.at[cuts[k]], dst.at[pl.ds(k * rows % D, rows)]))
        pltpu.make_async_copy(*outs[k], sem_out.at[k]).start()
    outs += [(pair.at[0], o_out), (pair.at[1], o_grad), (gain, o_gain)]
    for k in range(chunks, chunks + 3):
        loads[k].wait()
        pltpu.make_async_copy(*outs[k], sem_out.at[k]).start()
    for k in range(chunks + 3):
        pltpu.make_async_copy(*outs[k], sem_out.at[k]).wait()


def shards(Z, PL, C, nodes, adjacency, gain, w_in, w_out, cotangent):
    group, D = nodes.shape
    ppr = Z // C
    pc = group // C
    feat = D // C % 128 == 0
    gath = feat and C == 2 and D // PL % 128 == 0
    T = 2 if D // C // PL % (16 * Z) == 0 and not gath else 1
    w1 = 2 * D // C // T // PL
    spread = w1 % (16 * Z) == 0
    wz = w1 // Z if spread else w1
    if feat:
        field, piece = (Z * group, D // C), (PL - 1, group, D // C)
        split = split_in = (8, 128)
    else:
        field, piece = (ppr * group, D), (PL - 1, pc, D)
        split, split_in = (C, PL, pc, D), (C - 1, PL, pc, D)
    V = pltpu.VMEM
    S = pltpu.SemaphoreType.DMA

    def pair(n):
        return [S((n,)), S((n,))]

    scratch = [
        V((group, D), BF16), V((D, D), BF16), V((D, D), BF16), V((group, D), BF16),
        *([V((PL * group, Z * group), BF16)] if feat else [V((PL * group, ppr * group), BF16)]),
        V(field, BF16), V(field, BF16),
        V(split, F32), V(split_in, F32), V(piece, F32), V(piece, F32), V((group, D), F32),
        V(split, BF16), V(split_in, BF16), V(piece, BF16), V(piece, BF16), V((group, D), BF16),
        V((group, D), BF16), V((2, group, D), BF16), V((2, group, D), BF16),
        V((T, PL, w1, D), BF16), V((T * (PL - 1), w1, D), BF16),
        V((T, Z if spread else 1, wz, D), BF16), V((T, Z - 1 if spread else Z, wz, D), BF16),
        V((2 * D, D), BF16),
        V((8, D), F32), V((PL, 8, D), F32), V((Z, 8, D), F32), V((group, D), BF16), V((1, D), F32),
        V((PL * group, w1 if gath else 128), BF16), V((PL * group, D), BF16),
        S((4 + ppr,)), S((3 + T * PL * C,)),
        *pair((PL - 1) * ppr), *pair(PL * (C - 1)),
        S((Z - 1,)), S((Z - 1,)), S((Z - 1,)), S((Z - 1,)),
        *pair(PL * (C - 1)), *pair(PL - 1), *pair(C - 1),
        *pair(PL * (C - 1)), *pair(PL - 1), *pair(C - 1),
        *pair(T * (PL - 1)), *pair(T * (Z - 1)), *pair(T * (Z - 1)), *pair(T * (PL - 1)),
        *pair(T * PL * (C - 1)),
        *pair(PL - 1), *pair(Z - 1), *pair(PL - 1), *pair(PL - 1),
    ]
    H = pl.BlockSpec(memory_space=pltpu.HBM)
    M = pl.BlockSpec(memory_space=pltpu.VMEM)
    parts = pl.pallas_call(
        functools.partial(kernel, Z, PL, C, T, spread, feat, gath),
        out_shape=[
            jax.ShapeDtypeStruct((group, D), BF16),
            jax.ShapeDtypeStruct((group, D), BF16),
            jax.ShapeDtypeStruct((2 * D, D), BF16),
            jax.ShapeDtypeStruct((1, D), F32),
        ],
        in_specs=[H, H, M, H, H, H],
        out_specs=[H, H, H, H],
        scratch_shapes=scratch,
        compiler_params=pltpu.CompilerParams(
            collective_id=0, has_side_effects=True, vmem_limit_bytes=60 * 1024 * 1024
        ),
    )(nodes, adjacency, gain.reshape(1, D), w_in, w_out, cotangent)
    chunks = 8
    node_out, node_grad, g_in, g_out, gg = pl.pallas_call(
        functools.partial(closing, chunks),
        out_shape=[
            jax.ShapeDtypeStruct((group, D), BF16),
            jax.ShapeDtypeStruct((group, D), BF16),
            jax.ShapeDtypeStruct((D, D), F32),
            jax.ShapeDtypeStruct((D, D), F32),
            jax.ShapeDtypeStruct((1, D), F32),
        ],
        in_specs=[H, H, H, H],
        out_specs=[H, H, H, H, H],
        scratch_shapes=[
            V((2 * D, D), BF16), V((2 * D, D), F32), V((2, group, D), BF16), V((1, D), F32),
            S((chunks + 3,)), S((chunks + 3,)),
        ],
        compiler_params=pltpu.CompilerParams(vmem_limit_bytes=60 * 1024 * 1024),
    )(*parts)
    return node_out, node_grad, g_in, g_out, gg.reshape(D)


def solution(mesh):
    R, C = mesh.shape["rows"], mesh.shape["rep"]
    PL = math.isqrt(R)
    return jax.shard_map(
        functools.partial(shards, R // PL, PL, C),
        mesh=mesh,
        in_specs=(P("rows", None), P("rows", "rep"), P(), P(), P(), P("rows", None)),
        out_specs=(P("rows", None), P("rows", None), P(), P(), P()),
        check_vma=False,
    )
```

```python
import functools
import math

import jax
import jax.numpy as jnp
from jax import lax
from jax.experimental import pallas as pl
from jax.experimental.pallas import tpu as pltpu
from jax.sharding import PartitionSpec as P

MESH = pl.DeviceIdType.MESH
F32 = jnp.float32
BF16 = jnp.bfloat16


def dot(a, b, ca=1, cb=0):
    return lax.dot_general(a, b, (((ca,), (cb,)), ((), ())), preferred_element_type=F32)


def kernel(
    Z, PL, C, T, spread, feat, gath,
    nodes_h, adj_h, gain_ref, w_in_h, w_out_h, cot_h,
    node_out_h, node_grad_h, gw_h, gg_h,
    nodes, w_in, w_out, cot, a2, x, x2,
    part, cin, acc, pin, full, part2, cin2, acc2, pin2, full2,
    gs, lh, rh, gpart, gin, gz, gzin, gw, gg, ggp, ggz, no_v, gg_v, lall, rall,
    loc, st, a_s, a_r, ar_s, ar_r, x_s, x_r, x2_s, x2_r,
    c_s, c_r, p_s, p_r, f_s, f_r, c2_s, c2_r, p2_s, p2_r, f2_s, f2_r,
    g_s, g_r, z_s, z_r, zg_s, zg_r, pg_s, pg_r, rg_s, rg_r,
    ggp_s, ggp_r, ggz_s, ggz_r, l_s, l_r, ra_s, ra_r,
):
    g = lax.axis_index("rows")
    r = lax.axis_index("rep")
    z, p = lax.div(g, PL), lax.rem(g, PL)
    ppr = Z // C
    group, D = nodes.shape
    pc = group // C
    rows_w = 2 * D // C // T
    w1 = rows_w // PL
    wz = w1 // Z if spread else w1
    zl = lax.rem(z, ppr)
    owner = lax.div(z, ppr) == r
    lead = r * ppr if feat else 0
    Dc = D // C
    my_cols = pl.ds(pl.multiple_of(r * Dc, Dc), Dc)
    sends = []
    stores = []

    def store(src, dst):
        c = pltpu.make_async_copy(src, dst, st.at[len(stores)])
        c.start()
        stores.append(c)

    def z_peer(d):
        return {"rows": lax.rem(z + d, Z) * PL + p}

    def p_peer(d):
        return {"rows": z * PL + lax.rem(p + d, PL)}

    def r_peer(d):
        return {"rep": lax.rem(r + d, C)}

    def rcopy(src, dst, ss, rs, dev):
        return pltpu.make_async_remote_copy(
            src_ref=src, dst_ref=dst, send_sem=ss, recv_sem=rs, device_id=dev, device_id_type=MESH
        )

    def send(src, dst, ss, rs, dev):
        c = rcopy(src, dst, ss, rs, dev)
        c.start()
        sends.append(c)

    def arrived(dst, ss, rs, dev):
        rcopy(dst, dst, ss, rs, dev).wait_recv()

    def cols_of(k):
        return pl.ds(pl.multiple_of((lead + k) * group, group), group)

    own_cols = [
        pltpu.make_async_copy(
            adj_h.at[:, pl.ds(pl.multiple_of((k * PL + p) * group, group), group)],
            a2.at[pl.ds(pl.multiple_of(p * group, group), group), cols_of(k)],
            loc.at[4 + k],
        )
        for k in range(ppr)
    ]
    loads = [
        pltpu.make_async_copy(cot_h, cot, loc.at[0]),
        pltpu.make_async_copy(w_out_h, w_out, loc.at[1]),
        pltpu.make_async_copy(w_in_h, w_in, loc.at[2]),
        pltpu.make_async_copy(nodes_h, nodes, loc.at[3]),
    ]
    loads[3].start()
    for c in own_cols:
        c.start()
    for c in loads[:3]:
        c.start()

    barrier = pltpu.get_barrier_semaphore()
    for n, peer in ((Z, z_peer), (PL, p_peer), (C, r_peer)):
        for d in range(1, n):
            pl.semaphore_signal(barrier, inc=1, device_id=peer(d), device_id_type=MESH)
    loads[3].wait()
    pl.semaphore_wait(barrier, Z + PL + C - 3)

    def z_rows(k):
        return pl.ds(pl.multiple_of(k * group, group), group)

    def z_copies(src, buf, ss, rs):
        if feat:
            slot = buf.at[z_rows(z)]
            return [
                rcopy(src.at[:, my_cols], slot, ss.at[d - 1], rs.at[d - 1], z_peer(d))
                for d in range(1, Z)
            ]
        slot = buf.at[pl.ds(pl.multiple_of(zl * group, group), group)]
        return [rcopy(src, slot, ss.at[d - 1], rs.at[zl], z_peer(d)) for d in range(1, Z)]

    def z_start(src, buf, ss, rs):
        if feat:
            for c in z_copies(src, buf, ss, rs):
                c.start()
            buf[z_rows(z)] = src[:, my_cols]
            return

        @pl.when(owner)
        def _():
            for c in z_copies(src, buf, ss, rs):
                c.start()
            buf[pl.ds(pl.multiple_of(zl * group, group), group)] = src[...]

    def z_wait(src, buf, ss, rs):
        if feat:
            for d in range(1, Z):
                slot = buf.at[z_rows(lax.rem(z + Z - d, Z))]
                arrived(slot, ss.at[d - 1], rs.at[d - 1], z_peer(d))
            return
        for k in range(ppr):
            @pl.when(r * ppr + k != z)
            def _():
                arrived(buf.at[pl.ds(k * group, group)], ss.at[0], rs.at[k], z_peer(1))

    def z_drain(src, buf, ss, rs):
        if feat:
            for c in z_copies(src, buf, ss, rs):
                c.wait_send()
            return

        @pl.when(owner)
        def _():
            for c in z_copies(src, buf, ss, rs):
                c.wait_send()

    z_start(nodes, x, x_s, x_r)
    for d in range(1, PL):
        q = lax.rem(p + d, PL)
        for k in range(ppr):
            send(
                adj_h.at[:, pl.ds(pl.multiple_of((k * PL + q) * group, group), group)],
                a2.at[pl.ds(pl.multiple_of(p * group, group), group), cols_of(k)],
                a_s.at[(d - 1) * ppr + k], a_r.at[(d - 1) * ppr + k], p_peer(d),
            )

    def plane_copies(srcs, dst, ss, rs):
        slot = dst.at[z_rows(p)]
        return [rcopy(srcs(d), slot, ss.at[d - 1], rs.at[d - 1], p_peer(d)) for d in range(1, PL)]

    def left_copies(k):
        def cut(d):
            q = lax.rem(p + d, PL)
            return lh.at[k, :, pl.ds(pl.multiple_of(q * w1, w1), w1)]

        return plane_copies(cut, lall, l_s, l_r)

    def right_copies(src):
        return plane_copies(lambda d: src, rall, ra_s, ra_r)

    def begin(copies, core):
        @pl.when(r == core)
        def _():
            for c in copies():
                c.start()

    def end(copies, core):
        @pl.when(r == core)
        def _():
            for c in copies():
                c.wait_send()

    loads[0].wait()
    loads[1].wait()
    grad_hidden = dot(cot[...], w_out[...], 1, 1)
    loads[2].wait()
    for c in own_cols:
        c.wait()

    def halves(d, e):
        q = lax.rem(p + PL - d, PL)
        there = pl.multiple_of(lax.rem(r + C - e, C) * ppr * group, ppr * group)
        return a2.at[pl.ds(pl.multiple_of(q * group, group), group), pl.ds(there, ppr * group)]

    def forward(d):
        for e in range(1, C):
            i = d * (C - 1) + e - 1
            send(halves(d, 0), halves(d, 0), ar_s.at[i], ar_r.at[i], r_peer(e))

    if feat:
        forward(0)
    for d in range(1, PL):
        q = lax.rem(p + PL - d, PL)
        for k in range(ppr):
            arrived(
                a2.at[pl.ds(pl.multiple_of(q * group, group), group), cols_of(k)],
                a_s.at[(d - 1) * ppr + k], a_r.at[(d - 1) * ppr + k], p_peer(d),
            )
        if feat:
            forward(d)
    if feat:
        for d in range(PL):
            for e in range(1, C):
                i = d * (C - 1) + e - 1
                arrived(halves(d, e), ar_s.at[i], ar_r.at[i], r_peer(e))

    if gath:
        begin(lambda: right_copies(cot_h), 1)

    order = list(range(1, PL)) + [0]

    def partials(buf, out, ins, ss, rs):
        for d in order:
            q = lax.rem(p + d, PL)
            val = dot(a2[pl.ds(pl.multiple_of(q * group, group), group)], buf[...])
            for c in range(C):
                out[c, d] = val[c * pc:(c + 1) * pc].astype(out.dtype)
            for e in range(1, C):
                i = d * (C - 1) + e - 1
                send(out.at[lax.rem(r + e, C), d], ins.at[e - 1, d], ss.at[i], rs.at[i], r_peer(e))

    def combine(out, ins, ss, rs, accs, pins, pss, prs):
        for d in order:
            val = out[r, d].astype(F32)
            for e in range(1, C):
                i = d * (C - 1) + e - 1
                arrived(ins.at[e - 1, d], ss.at[i], rs.at[i], r_peer(e))
                val = val + ins[e - 1, d].astype(F32)
            if d == 0:
                return val
            accs[d - 1] = val.astype(accs.dtype)
            send(accs.at[d - 1], pins.at[d - 1], pss.at[d - 1], prs.at[d - 1], p_peer(d))

    def aggregate(buf, out, ins, ss, rs, accs, pins, pss, prs):
        if not feat:
            partials(buf, out, ins, ss, rs)
            return combine(out, ins, ss, rs, accs, pins, pss, prs)
        for d in order:
            q = lax.rem(p + d, PL)
            val = dot(a2[pl.ds(pl.multiple_of(q * group, group), group)], buf[...])
            if d == 0:
                return val
            accs[d - 1] = val.astype(accs.dtype)
            send(accs.at[d - 1], pins.at[d - 1], pss.at[d - 1], prs.at[d - 1], p_peer(d))

    def finish(val, accs, pins, pss, prs):
        for d in range(1, PL):
            arrived(pins.at[d - 1], pss.at[d - 1], prs.at[d - 1], p_peer(d))
            val = val + pins[d - 1].astype(F32)
        return val

    def piece_of(buf, c):
        if feat:
            return buf.at[:, pl.ds(pl.multiple_of(c * Dc, Dc), Dc)]
        return buf.at[pl.ds(pl.multiple_of(c * pc, pc), pc)]

    def share(buf, ss, rs):
        for d in range(1, C):
            send(piece_of(buf, r), piece_of(buf, r), ss.at[d - 1], rs.at[d - 1], r_peer(d))

    def shared(buf, ss, rs):
        for d in range(1, C):
            arrived(piece_of(buf, lax.rem(r + C - d, C)), ss.at[d - 1], rs.at[d - 1], r_peer(d))

    if feat:
        mine = (slice(None), my_cols)
    else:
        mine = pl.ds(pl.multiple_of(r * pc, pc), pc)
    z_wait(nodes, x, x_s, x_r)
    own = aggregate(x, part, cin, c_s, c_r, acc, pin, p_s, p_r)
    full[mine] = finish(own, acc, pin, p_s, p_r)
    share(full, f_s, f_r)
    shared(full, f_s, f_r)

    summed = full[...]
    gain = gain_ref[...]
    scale = lax.rsqrt(jnp.mean(summed * summed, axis=-1, keepdims=True) + 1e-05)
    normed = summed * scale
    lifted = (normed * gain).astype(BF16)
    lh[0] = lifted
    if gath:
        begin(lambda: left_copies(0), 0)
    pre = dot(lifted, w_in[...])
    sigma = jax.nn.sigmoid(pre)
    hidden = (pre * sigma).astype(BF16)

    def first_row(t, rep):
        if T == 1:
            return rep * rows_w
        return (1 - t) * D + rep * rows_w

    def weights_start(t, left, right):
        gval = dot(left, right, 0, 0)
        for q in range(PL):
            gpart[t, q] = gval[q * w1:(q + 1) * w1].astype(BF16)
        for d in range(1, PL):
            i = t * (PL - 1) + d - 1
            send(gpart.at[t, lax.rem(p + d, PL)], gin.at[i], g_s.at[i], g_r.at[i], p_peer(d))

    def columns(ref):
        return ref[:, pl.ds(pl.multiple_of(r * rows_w, rows_w), rows_w)]

    lh[1] = hidden
    if gath:
        begin(lambda: left_copies(1), 1)
    elif T == 2:
        weights_start(0, columns(lh.at[1]), cot[...])
    grad_pre = (grad_hidden * sigma * (1.0 + pre * (1.0 - sigma))).astype(BF16)
    rh[0] = grad_pre
    rh[1] = cot[...]
    if gath:
        begin(lambda: right_copies(rh.at[0]), 0)
    grad_lifted = dot(grad_pre, w_in[...], 1, 1)
    grad_normed = grad_lifted * gain
    gs[...] = (
        scale * (grad_normed - normed * jnp.mean(grad_normed * normed, axis=-1, keepdims=True))
    ).astype(BF16)
    z_start(gs, x2, x2_s, x2_r)

    if gath:
        lall[z_rows(p)] = lh[r, :, pl.ds(pl.multiple_of(p * w1, w1), w1)]
        rall[z_rows(p)] = rh[r]
    elif T == 2:
        weights_start(1, columns(lh.at[0]), grad_pre)
    else:
        half = C // 2
        which = lax.div(r, half)
        here = pl.multiple_of(lax.rem(r, half) * rows_w, rows_w)
        weights_start(0, lh[which, :, pl.ds(here, rows_w)], rh[which])
    gg[...] = jnp.broadcast_to(jnp.sum(grad_lifted * normed, axis=0, keepdims=True), gg.shape)
    ggp[p] = gg[...]
    for d in range(1, PL):
        send(gg, ggp.at[p], ggp_s.at[d - 1], ggp_r.at[d - 1], p_peer(d))
    no_v[...] = (nodes[...].astype(F32) + dot(hidden, w_out[...])).astype(BF16)
    store(no_v, node_out_h)

    def gw_rows(start, count):
        return gw.at[pl.ds(pl.multiple_of(start, count), count)]

    def scatter_z(t):
        if gath:
            for d in range(1, PL):
                slot = z_rows(lax.rem(p + PL - d, PL))
                arrived(lall.at[slot], l_s.at[d - 1], l_r.at[d - 1], p_peer(d))
                arrived(rall.at[slot], ra_s.at[d - 1], ra_r.at[d - 1], p_peer(d))
            gsum = dot(lall[...], rall[...], 0, 0)
        else:
            gsum = gpart[t, p].astype(F32)
            for d in range(1, PL):
                i = t * (PL - 1) + d - 1
                arrived(gin.at[i], g_s.at[i], g_r.at[i], p_peer(d))
                gsum = gsum + gin[i].astype(F32)
        if spread:
            for k in range(Z):
                gz[t, k] = gsum[k * wz:(k + 1) * wz].astype(BF16)
        else:
            gz[t, 0] = gsum.astype(BF16)
            gzin[t, z] = gz[t, 0]
        for d in range(1, Z):
            i = t * (Z - 1) + d - 1
            src = gz.at[t, lax.rem(z + d, Z)] if spread else gz.at[t, 0]
            dst = gzin.at[t, d - 1] if spread else gzin.at[t, z]
            send(src, dst, z_s.at[i], z_r.at[i], z_peer(d))

    def gather_z(t):
        base = first_row(t, r) + p * w1
        shard = gz[t, z].astype(F32) if spread else None
        for d in range(1, Z):
            i = t * (Z - 1) + d - 1
            slot = gzin.at[t, d - 1] if spread else gzin.at[t, lax.rem(z + Z - d, Z)]
            arrived(slot, z_s.at[i], z_r.at[i], z_peer(d))
            if spread:
                shard = shard + gzin[t, d - 1].astype(F32)
        if not spread:
            shard = gzin[t, 0].astype(F32)
            for k in range(1, Z):
                shard = shard + gzin[t, k].astype(F32)
            gw[pl.ds(pl.multiple_of(base, w1), w1)] = shard.astype(BF16)
            return
        here = base + z * wz
        gw[pl.ds(pl.multiple_of(here, wz), wz)] = shard.astype(BF16)
        for c in zg_copies(t):
            c.start()

    def zg_copies(t):
        if not spread:
            return []
        here = gw_rows(first_row(t, r) + p * w1 + z * wz, wz)
        first = t * (Z - 1) - 1
        return [rcopy(here, here, zg_s.at[first + d], zg_r.at[first + d], z_peer(d)) for d in range(1, Z)]

    def pg_copies(t):
        here = gw_rows(first_row(t, r) + p * w1, w1)
        first = t * (PL - 1) - 1
        return [rcopy(here, here, pg_s.at[first + d], pg_r.at[first + d], p_peer(d)) for d in range(1, PL)]

    def gather_plane(t):
        base = first_row(t, r) + p * w1
        if spread:
            for d in range(1, Z):
                i = t * (Z - 1) + d - 1
                there = base + lax.rem(z + Z - d, Z) * wz
                arrived(gw_rows(there, wz), zg_s.at[i], zg_r.at[i], z_peer(d))
        for c in pg_copies(t):
            c.start()

    def keep(start):
        store(gw_rows(start, w1), gw_h.at[pl.ds(pl.multiple_of(start, w1), w1)])

    def gather_rep(t):
        for d in range(PL):
            start = first_row(t, r) + lax.rem(p + PL - d, PL) * w1
            block = gw_rows(start, w1)
            if d > 0:
                i = t * (PL - 1) + d - 1
                arrived(block, pg_s.at[i], pg_r.at[i], p_peer(d))
            for e in range(1, C):
                i = (t * PL + d) * (C - 1) + e - 1
                send(block, block, rg_s.at[i], rg_r.at[i], r_peer(e))
            keep(start)

    def gather_end(t):
        for d in range(PL):
            for e in range(1, C):
                i = (t * PL + d) * (C - 1) + e - 1
                start = first_row(t, lax.rem(r + C - e, C)) + lax.rem(p + PL - d, PL) * w1
                arrived(gw_rows(start, w1), rg_s.at[i], rg_r.at[i], r_peer(e))
                keep(start)

    last = T - 1
    for t in range(T):
        scatter_z(t)
    if gath:
        @pl.when(r == 1)
        def _():
            gather_z(0)
    elif T == 2:
        gather_z(0)
    z_wait(gs, x2, x2_s, x2_r)
    own2 = aggregate(x2, part2, cin2, c2_s, c2_r, acc2, pin2, p2_s, p2_r)
    if gath:
        @pl.when(r == 1)
        def _():
            gather_plane(0)

        @pl.when(r == 0)
        def _():
            gather_z(0)
            gather_plane(0)
    else:
        gather_z(last)
        for t in range(T):
            gather_plane(t)

    for d in range(1, PL):
        arrived(ggp.at[lax.rem(p + PL - d, PL)], ggp_s.at[d - 1], ggp_r.at[d - 1], p_peer(d))
    ggv = ggp[0]
    for q in range(1, PL):
        ggv = ggv + ggp[q]
    ggz[z] = ggv
    for d in range(1, Z):
        send(ggz.at[z], ggz.at[z], ggz_s.at[d - 1], ggz_r.at[d - 1], z_peer(d))

    back = finish(own2, acc2, pin2, p2_s, p2_r)
    full2[mine] = (cot[mine].astype(F32) + back).astype(BF16)
    share(full2, f2_s, f2_r)
    gather_rep(0)
    shared(full2, f2_s, f2_r)
    store(full2, node_grad_h)
    if T == 2:
        gather_rep(1)
    for d in range(1, Z):
        arrived(ggz.at[lax.rem(z + Z - d, Z)], ggz_s.at[d - 1], ggz_r.at[d - 1], z_peer(d))
    ggv = ggz[0]
    for k in range(1, Z):
        ggv = ggv + ggz[k]
    gg_v[...] = ggv[:1]
    store(gg_v, gg_h)
    for t in range(T):
        gather_end(t)
    for c in sends:
        c.wait_send()
    for t in range(T):
        for c in zg_copies(t) + pg_copies(t):
            c.wait_send()
    if gath:
        end(lambda: left_copies(0) + right_copies(rh.at[0]), 0)
        end(lambda: left_copies(1) + right_copies(cot_h), 1)
    z_drain(nodes, x, x_s, x_r)
    z_drain(gs, x2, x2_s, x2_r)
    for c in stores:
        c.wait()


def closing(
    chunks, node_out, node_grad, gw, gg, o_out, o_grad, o_win, o_wout, o_gain,
    narrow, wide, pair, gain, sem_in, sem_out,
):
    D = o_win.shape[0]
    rows = 2 * D // chunks
    cuts = [pl.ds(k * rows, rows) for k in range(chunks)]
    steps = [(gw.at[c], narrow.at[c]) for c in cuts]
    steps += [(node_out, pair.at[0]), (node_grad, pair.at[1]), (gg, gain)]
    loads = [pltpu.make_async_copy(a, b, sem_in.at[i]) for i, (a, b) in enumerate(steps)]
    for c in loads:
        c.start()
    outs = []
    for k in range(chunks):
        loads[k].wait()
        wide[cuts[k]] = narrow[cuts[k]].astype(F32)
        dst = o_win if k * rows < D else o_wout
        outs.append((wide.at[cuts[k]], dst.at[pl.ds(k * rows % D, rows)]))
        pltpu.make_async_copy(*outs[k], sem_out.at[k]).start()
    outs += [(pair.at[0], o_out), (pair.at[1], o_grad), (gain, o_gain)]
    for k in range(chunks, chunks + 3):
        loads[k].wait()
        pltpu.make_async_copy(*outs[k], sem_out.at[k]).start()
    for k in range(chunks + 3):
        pltpu.make_async_copy(*outs[k], sem_out.at[k]).wait()


def shards(Z, PL, C, nodes, adjacency, gain, w_in, w_out, cotangent):
    group, D = nodes.shape
    ppr = Z // C
    pc = group // C
    feat = D // C % 128 == 0
    gath = feat and C == 2 and D // PL % 128 == 0
    T = 2 if D // C // PL % (16 * Z) == 0 and not gath else 1
    w1 = 2 * D // C // T // PL
    spread = w1 % (16 * Z) == 0
    wz = w1 // Z if spread else w1
    if feat:
        field, piece = (Z * group, D // C), (PL - 1, group, D // C)
        split = split_in = (8, 128)
    else:
        field, piece = (ppr * group, D), (PL - 1, pc, D)
        split, split_in = (C, PL, pc, D), (C - 1, PL, pc, D)
    V = pltpu.VMEM
    S = pltpu.SemaphoreType.DMA

    def pair(n):
        return [S((n,)), S((n,))]

    scratch = [
        V((group, D), BF16), V((D, D), BF16), V((D, D), BF16), V((group, D), BF16),
        *([V((PL * group, Z * group), BF16)] if feat else [V((PL * group, ppr * group), BF16)]),
        V(field, BF16), V(field, BF16),
        V(split, F32), V(split_in, F32), V(piece, F32), V(piece, F32), V((group, D), F32),
        V(split, BF16), V(split_in, BF16), V(piece, BF16), V(piece, BF16), V((group, D), BF16),
        V((group, D), BF16), V((2, group, D), BF16), V((2, group, D), BF16),
        V((T, PL, w1, D), BF16), V((T * (PL - 1), w1, D), BF16),
        V((T, Z if spread else 1, wz, D), BF16), V((T, Z - 1 if spread else Z, wz, D), BF16),
        V((2 * D, D), BF16),
        V((8, D), F32), V((PL, 8, D), F32), V((Z, 8, D), F32), V((group, D), BF16), V((1, D), F32),
        V((PL * group, w1 if gath else 128), BF16), V((PL * group, D), BF16),
        S((4 + ppr,)), S((3 + T * PL * C,)),
        *pair((PL - 1) * ppr), *pair(PL * (C - 1)),
        S((Z - 1,)), S((Z - 1,)), S((Z - 1,)), S((Z - 1,)),
        *pair(PL * (C - 1)), *pair(PL - 1), *pair(C - 1),
        *pair(PL * (C - 1)), *pair(PL - 1), *pair(C - 1),
        *pair(T * (PL - 1)), *pair(T * (Z - 1)), *pair(T * (Z - 1)), *pair(T * (PL - 1)),
        *pair(T * PL * (C - 1)),
        *pair(PL - 1), *pair(Z - 1), *pair(PL - 1), *pair(PL - 1),
    ]
    H = pl.BlockSpec(memory_space=pltpu.HBM)
    M = pl.BlockSpec(memory_space=pltpu.VMEM)
    parts = pl.pallas_call(
        functools.partial(kernel, Z, PL, C, T, spread, feat, gath),
        out_shape=[
            jax.ShapeDtypeStruct((group, D), BF16),
            jax.ShapeDtypeStruct((group, D), BF16),
            jax.ShapeDtypeStruct((2 * D, D), BF16),
            jax.ShapeDtypeStruct((1, D), F32),
        ],
        in_specs=[H, H, M, H, H, H],
        out_specs=[H, H, H, H],
        scratch_shapes=scratch,
        compiler_params=pltpu.CompilerParams(
            collective_id=0, has_side_effects=True, vmem_limit_bytes=60 * 1024 * 1024
        ),
    )(nodes, adjacency, gain.reshape(1, D), w_in, w_out, cotangent)
    chunks = 8
    node_out, node_grad, g_in, g_out, gg = pl.pallas_call(
        functools.partial(closing, chunks),
        out_shape=[
            jax.ShapeDtypeStruct((group, D), BF16),
            jax.ShapeDtypeStruct((group, D), BF16),
            jax.ShapeDtypeStruct((D, D), F32),
            jax.ShapeDtypeStruct((D, D), F32),
            jax.ShapeDtypeStruct((1, D), F32),
        ],
        in_specs=[H, H, H, H],
        out_specs=[H, H, H, H, H],
        scratch_shapes=[
            V((2 * D, D), BF16), V((2 * D, D), F32), V((2, group, D), BF16), V((1, D), F32),
            S((chunks + 3,)), S((chunks + 3,)),
        ],
        compiler_params=pltpu.CompilerParams(vmem_limit_bytes=60 * 1024 * 1024),
    )(*parts)
    return node_out, node_grad, g_in, g_out, gg.reshape(D)


def solution(mesh):
    R, C = mesh.shape["rows"], mesh.shape["rep"]
    PL = math.isqrt(R)
    return jax.shard_map(
        functools.partial(shards, R // PL, PL, C),
        mesh=mesh,
        in_specs=(P("rows", None), P("rows", "rep"), P(), P(), P(), P("rows", None)),
        out_specs=(P("rows", None), P("rows", None), P(), P(), P()),
        check_vma=False,
    )
```

```python
import functools
import math

import jax
import jax.numpy as jnp
from jax import lax
from jax.experimental import pallas as pl
from jax.experimental.pallas import tpu as pltpu
from jax.sharding import PartitionSpec as P

MESH = pl.DeviceIdType.MESH
F32 = jnp.float32
BF16 = jnp.bfloat16


def dot(a, b, ca=1, cb=0):
    return lax.dot_general(a, b, (((ca,), (cb,)), ((), ())), preferred_element_type=F32)


def kernel(
    Z, PL, C, T, spread, feat,
    nodes_h, adj_h, gain_ref, w_in_h, w_out_h, cot_h,
    node_out_h, node_grad_h, gw_h, gg_h,
    nodes, w_in, w_out, cot, a2, x, x2,
    part, cin, acc, pin, full, part2, cin2, acc2, pin2, full2,
    gs, lh, rh, gpart, gin, gz, gzin, gw, gg, ggp, ggz, no_v, gg_v,
    loc, st, a_s, a_r, ar_s, ar_r, x_s, x_r, x2_s, x2_r,
    c_s, c_r, p_s, p_r, f_s, f_r, c2_s, c2_r, p2_s, p2_r, f2_s, f2_r,
    g_s, g_r, z_s, z_r, zg_s, zg_r, pg_s, pg_r, rg_s, rg_r,
    ggp_s, ggp_r, ggz_s, ggz_r,
):
    g = lax.axis_index("rows")
    r = lax.axis_index("rep")
    z, p = lax.div(g, PL), lax.rem(g, PL)
    ppr = Z // C
    group, D = nodes.shape
    pc = group // C
    rows_w = 2 * D // C // T
    w1 = rows_w // PL
    wz = w1 // Z if spread else w1
    zl = lax.rem(z, ppr)
    owner = lax.div(z, ppr) == r
    lead = r * ppr if feat else 0
    Dc = D // C
    my_cols = pl.ds(pl.multiple_of(r * Dc, Dc), Dc)
    sends = []
    stores = []

    def store(src, dst):
        c = pltpu.make_async_copy(src, dst, st.at[len(stores)])
        c.start()
        stores.append(c)

    def z_peer(d):
        return {"rows": lax.rem(z + d, Z) * PL + p}

    def p_peer(d):
        return {"rows": z * PL + lax.rem(p + d, PL)}

    def r_peer(d):
        return {"rep": lax.rem(r + d, C)}

    def rcopy(src, dst, ss, rs, dev):
        return pltpu.make_async_remote_copy(
            src_ref=src, dst_ref=dst, send_sem=ss, recv_sem=rs, device_id=dev, device_id_type=MESH
        )

    def send(src, dst, ss, rs, dev):
        c = rcopy(src, dst, ss, rs, dev)
        c.start()
        sends.append(c)

    def arrived(dst, ss, rs, dev):
        rcopy(dst, dst, ss, rs, dev).wait_recv()

    def cols_of(k):
        return pl.ds(pl.multiple_of((lead + k) * group, group), group)

    own_cols = [
        pltpu.make_async_copy(
            adj_h.at[:, pl.ds(pl.multiple_of((k * PL + p) * group, group), group)],
            a2.at[pl.ds(pl.multiple_of(p * group, group), group), cols_of(k)],
            loc.at[4 + k],
        )
        for k in range(ppr)
    ]
    loads = [
        pltpu.make_async_copy(cot_h, cot, loc.at[0]),
        pltpu.make_async_copy(w_out_h, w_out, loc.at[1]),
        pltpu.make_async_copy(w_in_h, w_in, loc.at[2]),
        pltpu.make_async_copy(nodes_h, nodes, loc.at[3]),
    ]
    loads[3].start()
    for c in own_cols:
        c.start()
    for c in loads[:3]:
        c.start()

    barrier = pltpu.get_barrier_semaphore()
    for n, peer in ((Z, z_peer), (PL, p_peer), (C, r_peer)):
        for d in range(1, n):
            pl.semaphore_signal(barrier, inc=1, device_id=peer(d), device_id_type=MESH)
    loads[3].wait()
    pl.semaphore_wait(barrier, Z + PL + C - 3)

    def z_rows(k):
        return pl.ds(pl.multiple_of(k * group, group), group)

    def z_copies(src, buf, ss, rs):
        if feat:
            slot = buf.at[z_rows(z)]
            return [
                rcopy(src.at[:, my_cols], slot, ss.at[d - 1], rs.at[d - 1], z_peer(d))
                for d in range(1, Z)
            ]
        slot = buf.at[pl.ds(pl.multiple_of(zl * group, group), group)]
        return [rcopy(src, slot, ss.at[d - 1], rs.at[zl], z_peer(d)) for d in range(1, Z)]

    def z_start(src, buf, ss, rs):
        if feat:
            for c in z_copies(src, buf, ss, rs):
                c.start()
            buf[z_rows(z)] = src[:, my_cols]
            return

        @pl.when(owner)
        def _():
            for c in z_copies(src, buf, ss, rs):
                c.start()
            buf[pl.ds(pl.multiple_of(zl * group, group), group)] = src[...]

    def z_wait(src, buf, ss, rs):
        if feat:
            for d in range(1, Z):
                slot = buf.at[z_rows(lax.rem(z + Z - d, Z))]
                arrived(slot, ss.at[d - 1], rs.at[d - 1], z_peer(d))
            return
        for k in range(ppr):
            @pl.when(r * ppr + k != z)
            def _():
                arrived(buf.at[pl.ds(k * group, group)], ss.at[0], rs.at[k], z_peer(1))

    def z_drain(src, buf, ss, rs):
        if feat:
            for c in z_copies(src, buf, ss, rs):
                c.wait_send()
            return

        @pl.when(owner)
        def _():
            for c in z_copies(src, buf, ss, rs):
                c.wait_send()

    z_start(nodes, x, x_s, x_r)
    for d in range(1, PL):
        q = lax.rem(p + d, PL)
        for k in range(ppr):
            send(
                adj_h.at[:, pl.ds(pl.multiple_of((k * PL + q) * group, group), group)],
                a2.at[pl.ds(pl.multiple_of(p * group, group), group), cols_of(k)],
                a_s.at[(d - 1) * ppr + k], a_r.at[(d - 1) * ppr + k], p_peer(d),
            )

    loads[0].wait()
    loads[1].wait()
    grad_hidden = dot(cot[...], w_out[...], 1, 1)
    loads[2].wait()
    for c in own_cols:
        c.wait()

    def halves(d, e):
        q = lax.rem(p + PL - d, PL)
        there = pl.multiple_of(lax.rem(r + C - e, C) * ppr * group, ppr * group)
        return a2.at[pl.ds(pl.multiple_of(q * group, group), group), pl.ds(there, ppr * group)]

    def forward(d):
        for e in range(1, C):
            i = d * (C - 1) + e - 1
            send(halves(d, 0), halves(d, 0), ar_s.at[i], ar_r.at[i], r_peer(e))

    if feat:
        forward(0)
    for d in range(1, PL):
        q = lax.rem(p + PL - d, PL)
        for k in range(ppr):
            arrived(
                a2.at[pl.ds(pl.multiple_of(q * group, group), group), cols_of(k)],
                a_s.at[(d - 1) * ppr + k], a_r.at[(d - 1) * ppr + k], p_peer(d),
            )
        if feat:
            forward(d)
    if feat:
        for d in range(PL):
            for e in range(1, C):
                i = d * (C - 1) + e - 1
                arrived(halves(d, e), ar_s.at[i], ar_r.at[i], r_peer(e))

    order = list(range(1, PL)) + [0]

    def partials(buf, out, ins, ss, rs):
        for d in order:
            q = lax.rem(p + d, PL)
            val = dot(a2[pl.ds(pl.multiple_of(q * group, group), group)], buf[...])
            for c in range(C):
                out[c, d] = val[c * pc:(c + 1) * pc].astype(out.dtype)
            for e in range(1, C):
                i = d * (C - 1) + e - 1
                send(out.at[lax.rem(r + e, C), d], ins.at[e - 1, d], ss.at[i], rs.at[i], r_peer(e))

    def combine(out, ins, ss, rs, accs, pins, pss, prs):
        for d in order:
            val = out[r, d].astype(F32)
            for e in range(1, C):
                i = d * (C - 1) + e - 1
                arrived(ins.at[e - 1, d], ss.at[i], rs.at[i], r_peer(e))
                val = val + ins[e - 1, d].astype(F32)
            if d == 0:
                return val
            accs[d - 1] = val.astype(accs.dtype)
            send(accs.at[d - 1], pins.at[d - 1], pss.at[d - 1], prs.at[d - 1], p_peer(d))

    def aggregate(buf, out, ins, ss, rs, accs, pins, pss, prs):
        if not feat:
            partials(buf, out, ins, ss, rs)
            return combine(out, ins, ss, rs, accs, pins, pss, prs)
        for d in order:
            q = lax.rem(p + d, PL)
            val = dot(a2[pl.ds(pl.multiple_of(q * group, group), group)], buf[...])
            if d == 0:
                return val
            accs[d - 1] = val.astype(accs.dtype)
            send(accs.at[d - 1], pins.at[d - 1], pss.at[d - 1], prs.at[d - 1], p_peer(d))

    def finish(val, accs, pins, pss, prs):
        for d in range(1, PL):
            arrived(pins.at[d - 1], pss.at[d - 1], prs.at[d - 1], p_peer(d))
            val = val + pins[d - 1].astype(F32)
        return val

    def piece_of(buf, c):
        if feat:
            return buf.at[:, pl.ds(pl.multiple_of(c * Dc, Dc), Dc)]
        return buf.at[pl.ds(pl.multiple_of(c * pc, pc), pc)]

    def share(buf, ss, rs):
        for d in range(1, C):
            send(piece_of(buf, r), piece_of(buf, r), ss.at[d - 1], rs.at[d - 1], r_peer(d))

    def shared(buf, ss, rs):
        for d in range(1, C):
            arrived(piece_of(buf, lax.rem(r + C - d, C)), ss.at[d - 1], rs.at[d - 1], r_peer(d))

    if feat:
        mine = (slice(None), my_cols)
    else:
        mine = pl.ds(pl.multiple_of(r * pc, pc), pc)
    z_wait(nodes, x, x_s, x_r)
    own = aggregate(x, part, cin, c_s, c_r, acc, pin, p_s, p_r)
    full[mine] = finish(own, acc, pin, p_s, p_r)
    share(full, f_s, f_r)
    shared(full, f_s, f_r)

    summed = full[...]
    gain = gain_ref[...]
    scale = lax.rsqrt(jnp.mean(summed * summed, axis=-1, keepdims=True) + 1e-05)
    normed = summed * scale
    lifted = (normed * gain).astype(BF16)
    pre = dot(lifted, w_in[...])
    sigma = jax.nn.sigmoid(pre)
    hidden = (pre * sigma).astype(BF16)

    def first_row(t, rep):
        if T == 1:
            return rep * rows_w
        return (1 - t) * D + rep * rows_w

    def weights_start(t, left, right):
        gval = dot(left, right, 0, 0)
        for q in range(PL):
            gpart[t, q] = gval[q * w1:(q + 1) * w1].astype(BF16)
        for d in range(1, PL):
            i = t * (PL - 1) + d - 1
            send(gpart.at[t, lax.rem(p + d, PL)], gin.at[i], g_s.at[i], g_r.at[i], p_peer(d))

    def columns(ref):
        return ref[:, pl.ds(pl.multiple_of(r * rows_w, rows_w), rows_w)]

    lh[1] = hidden
    grad_pre = (grad_hidden * sigma * (1.0 + pre * (1.0 - sigma))).astype(BF16)
    grad_lifted = dot(grad_pre, w_in[...], 1, 1)
    grad_normed = grad_lifted * gain
    gs[...] = (
        scale * (grad_normed - normed * jnp.mean(grad_normed * normed, axis=-1, keepdims=True))
    ).astype(BF16)
    z_start(gs, x2, x2_s, x2_r)

    lh[0] = lifted
    if T == 2:
        weights_start(0, columns(lh.at[1]), cot[...])
        weights_start(1, columns(lh.at[0]), grad_pre)
    else:
        rh[0] = grad_pre
        rh[1] = cot[...]
        half = C // 2
        which = lax.div(r, half)
        here = pl.multiple_of(lax.rem(r, half) * rows_w, rows_w)
        weights_start(0, lh[which, :, pl.ds(here, rows_w)], rh[which])
    gg[...] = jnp.broadcast_to(jnp.sum(grad_lifted * normed, axis=0, keepdims=True), gg.shape)
    ggp[p] = gg[...]
    for d in range(1, PL):
        send(gg, ggp.at[p], ggp_s.at[d - 1], ggp_r.at[d - 1], p_peer(d))
    no_v[...] = (nodes[...].astype(F32) + dot(hidden, w_out[...])).astype(BF16)
    store(no_v, node_out_h)

    def gw_rows(start, count):
        return gw.at[pl.ds(pl.multiple_of(start, count), count)]

    def scatter_z(t):
        gsum = gpart[t, p].astype(F32)
        for d in range(1, PL):
            i = t * (PL - 1) + d - 1
            arrived(gin.at[i], g_s.at[i], g_r.at[i], p_peer(d))
            gsum = gsum + gin[i].astype(F32)
        if spread:
            for k in range(Z):
                gz[t, k] = gsum[k * wz:(k + 1) * wz].astype(BF16)
        else:
            gz[t, 0] = gsum.astype(BF16)
            gzin[t, z] = gz[t, 0]
        for d in range(1, Z):
            i = t * (Z - 1) + d - 1
            src = gz.at[t, lax.rem(z + d, Z)] if spread else gz.at[t, 0]
            dst = gzin.at[t, d - 1] if spread else gzin.at[t, z]
            send(src, dst, z_s.at[i], z_r.at[i], z_peer(d))

    def gather_z(t):
        base = first_row(t, r) + p * w1
        shard = gz[t, z].astype(F32) if spread else None
        for d in range(1, Z):
            i = t * (Z - 1) + d - 1
            slot = gzin.at[t, d - 1] if spread else gzin.at[t, lax.rem(z + Z - d, Z)]
            arrived(slot, z_s.at[i], z_r.at[i], z_peer(d))
            if spread:
                shard = shard + gzin[t, d - 1].astype(F32)
        if not spread:
            shard = gzin[t, 0].astype(F32)
            for k in range(1, Z):
                shard = shard + gzin[t, k].astype(F32)
            gw[pl.ds(pl.multiple_of(base, w1), w1)] = shard.astype(BF16)
            return
        here = base + z * wz
        gw[pl.ds(pl.multiple_of(here, wz), wz)] = shard.astype(BF16)
        for d in range(1, Z):
            i = t * (Z - 1) + d - 1
            send(gw_rows(here, wz), gw_rows(here, wz), zg_s.at[i], zg_r.at[i], z_peer(d))

    def gather_plane(t):
        base = first_row(t, r) + p * w1
        if spread:
            for d in range(1, Z):
                i = t * (Z - 1) + d - 1
                there = base + lax.rem(z + Z - d, Z) * wz
                arrived(gw_rows(there, wz), zg_s.at[i], zg_r.at[i], z_peer(d))
        for d in range(1, PL):
            i = t * (PL - 1) + d - 1
            send(gw_rows(base, w1), gw_rows(base, w1), pg_s.at[i], pg_r.at[i], p_peer(d))

    def keep(start):
        store(gw_rows(start, w1), gw_h.at[pl.ds(pl.multiple_of(start, w1), w1)])

    def gather_rep(t):
        for d in range(PL):
            start = first_row(t, r) + lax.rem(p + PL - d, PL) * w1
            block = gw_rows(start, w1)
            if d > 0:
                i = t * (PL - 1) + d - 1
                arrived(block, pg_s.at[i], pg_r.at[i], p_peer(d))
            for e in range(1, C):
                i = (t * PL + d) * (C - 1) + e - 1
                send(block, block, rg_s.at[i], rg_r.at[i], r_peer(e))
            keep(start)

    def gather_end(t):
        for d in range(PL):
            for e in range(1, C):
                i = (t * PL + d) * (C - 1) + e - 1
                start = first_row(t, lax.rem(r + C - e, C)) + lax.rem(p + PL - d, PL) * w1
                arrived(gw_rows(start, w1), rg_s.at[i], rg_r.at[i], r_peer(e))
                keep(start)

    last = T - 1
    for t in range(T):
        scatter_z(t)
    if T == 2:
        gather_z(0)
    z_wait(gs, x2, x2_s, x2_r)
    own2 = aggregate(x2, part2, cin2, c2_s, c2_r, acc2, pin2, p2_s, p2_r)
    gather_z(last)
    for t in range(T):
        gather_plane(t)

    for d in range(1, PL):
        arrived(ggp.at[lax.rem(p + PL - d, PL)], ggp_s.at[d - 1], ggp_r.at[d - 1], p_peer(d))
    ggv = ggp[0]
    for q in range(1, PL):
        ggv = ggv + ggp[q]
    ggz[z] = ggv
    for d in range(1, Z):
        send(ggz.at[z], ggz.at[z], ggz_s.at[d - 1], ggz_r.at[d - 1], z_peer(d))

    back = finish(own2, acc2, pin2, p2_s, p2_r)
    full2[mine] = (cot[mine].astype(F32) + back).astype(BF16)
    share(full2, f2_s, f2_r)
    gather_rep(0)
    shared(full2, f2_s, f2_r)
    store(full2, node_grad_h)
    if T == 2:
        gather_rep(1)
    for d in range(1, Z):
        arrived(ggz.at[lax.rem(z + Z - d, Z)], ggz_s.at[d - 1], ggz_r.at[d - 1], z_peer(d))
    ggv = ggz[0]
    for k in range(1, Z):
        ggv = ggv + ggz[k]
    gg_v[...] = ggv[:1]
    store(gg_v, gg_h)
    for t in range(T):
        gather_end(t)
    for c in sends:
        c.wait_send()
    z_drain(nodes, x, x_s, x_r)
    z_drain(gs, x2, x2_s, x2_r)
    for c in stores:
        c.wait()


def closing(
    chunks, node_out, node_grad, gw, gg, o_out, o_grad, o_win, o_wout, o_gain,
    narrow, wide, pair, gain, sem_in, sem_out,
):
    D = o_win.shape[0]
    rows = 2 * D // chunks
    cuts = [pl.ds(k * rows, rows) for k in range(chunks)]
    steps = [(gw.at[c], narrow.at[c]) for c in cuts]
    steps += [(node_out, pair.at[0]), (node_grad, pair.at[1]), (gg, gain)]
    loads = [pltpu.make_async_copy(a, b, sem_in.at[i]) for i, (a, b) in enumerate(steps)]
    for c in loads:
        c.start()
    outs = []
    for k in range(chunks):
        loads[k].wait()
        wide[cuts[k]] = narrow[cuts[k]].astype(F32)
        dst = o_win if k * rows < D else o_wout
        outs.append((wide.at[cuts[k]], dst.at[pl.ds(k * rows % D, rows)]))
        pltpu.make_async_copy(*outs[k], sem_out.at[k]).start()
    outs += [(pair.at[0], o_out), (pair.at[1], o_grad), (gain, o_gain)]
    for k in range(chunks, chunks + 3):
        loads[k].wait()
        pltpu.make_async_copy(*outs[k], sem_out.at[k]).start()
    for k in range(chunks + 3):
        pltpu.make_async_copy(*outs[k], sem_out.at[k]).wait()


def shards(Z, PL, C, nodes, adjacency, gain, w_in, w_out, cotangent):
    group, D = nodes.shape
    ppr = Z // C
    pc = group // C
    feat = D // C % 128 == 0
    T = 2 if D // C // PL % (16 * Z) == 0 else 1
    w1 = 2 * D // C // T // PL
    spread = w1 % (16 * Z) == 0
    wz = w1 // Z if spread else w1
    if feat:
        field, piece = (Z * group, D // C), (PL - 1, group, D // C)
        split = split_in = (8, 128)
    else:
        field, piece = (ppr * group, D), (PL - 1, pc, D)
        split, split_in = (C, PL, pc, D), (C - 1, PL, pc, D)
    V = pltpu.VMEM
    S = pltpu.SemaphoreType.DMA

    def pair(n):
        return [S((n,)), S((n,))]

    scratch = [
        V((group, D), BF16), V((D, D), BF16), V((D, D), BF16), V((group, D), BF16),
        *([V((PL * group, Z * group), BF16)] if feat else [V((PL * group, ppr * group), BF16)]),
        V(field, BF16), V(field, BF16),
        V(split, F32), V(split_in, F32), V(piece, BF16), V(piece, BF16), V((group, D), F32),
        V(split, BF16), V(split_in, BF16), V(piece, BF16), V(piece, BF16), V((group, D), BF16),
        V((group, D), BF16), V((2, group, D), BF16), V((2, group, D), BF16),
        V((T, PL, w1, D), BF16), V((T * (PL - 1), w1, D), BF16),
        V((T, Z if spread else 1, wz, D), BF16), V((T, Z - 1 if spread else Z, wz, D), BF16),
        V((2 * D, D), BF16),
        V((8, D), F32), V((PL, 8, D), F32), V((Z, 8, D), F32), V((group, D), BF16), V((1, D), F32),
        S((4 + ppr,)), S((3 + T * PL * C,)),
        *pair((PL - 1) * ppr), *pair(PL * (C - 1)),
        S((Z - 1,)), S((Z - 1,)), S((Z - 1,)), S((Z - 1,)),
        *pair(PL * (C - 1)), *pair(PL - 1), *pair(C - 1),
        *pair(PL * (C - 1)), *pair(PL - 1), *pair(C - 1),
        *pair(T * (PL - 1)), *pair(T * (Z - 1)), *pair(T * (Z - 1)), *pair(T * (PL - 1)),
        *pair(T * PL * (C - 1)),
        *pair(PL - 1), *pair(Z - 1),
    ]
    H = pl.BlockSpec(memory_space=pltpu.HBM)
    M = pl.BlockSpec(memory_space=pltpu.VMEM)
    parts = pl.pallas_call(
        functools.partial(kernel, Z, PL, C, T, spread, feat),
        out_shape=[
            jax.ShapeDtypeStruct((group, D), BF16),
            jax.ShapeDtypeStruct((group, D), BF16),
            jax.ShapeDtypeStruct((2 * D, D), BF16),
            jax.ShapeDtypeStruct((1, D), F32),
        ],
        in_specs=[H, H, M, H, H, H],
        out_specs=[H, H, H, H],
        scratch_shapes=scratch,
        compiler_params=pltpu.CompilerParams(
            collective_id=0, has_side_effects=True, vmem_limit_bytes=60 * 1024 * 1024
        ),
    )(nodes, adjacency, gain.reshape(1, D), w_in, w_out, cotangent)
    chunks = 8
    node_out, node_grad, g_in, g_out, gg = pl.pallas_call(
        functools.partial(closing, chunks),
        out_shape=[
            jax.ShapeDtypeStruct((group, D), BF16),
            jax.ShapeDtypeStruct((group, D), BF16),
            jax.ShapeDtypeStruct((D, D), F32),
            jax.ShapeDtypeStruct((D, D), F32),
            jax.ShapeDtypeStruct((1, D), F32),
        ],
        in_specs=[H, H, H, H],
        out_specs=[H, H, H, H, H],
        scratch_shapes=[
            V((2 * D, D), BF16), V((2 * D, D), F32), V((2, group, D), BF16), V((1, D), F32),
            S((chunks + 3,)), S((chunks + 3,)),
        ],
        compiler_params=pltpu.CompilerParams(vmem_limit_bytes=60 * 1024 * 1024),
    )(*parts)
    return node_out, node_grad, g_in, g_out, gg.reshape(D)


def solution(mesh):
    R, C = mesh.shape["rows"], mesh.shape["rep"]
    PL = math.isqrt(R)
    return jax.shard_map(
        functools.partial(shards, R // PL, PL, C),
        mesh=mesh,
        in_specs=(P("rows", None), P("rows", "rep"), P(), P(), P(), P("rows", None)),
        out_specs=(P("rows", None), P("rows", None), P(), P(), P()),
        check_vma=False,
    )
```

```python
import functools
import math

import jax
import jax.numpy as jnp
from jax import lax
from jax.experimental import pallas as pl
from jax.experimental.pallas import tpu as pltpu
from jax.sharding import PartitionSpec as P

MESH = pl.DeviceIdType.MESH
F32 = jnp.float32
BF16 = jnp.bfloat16


def dot(a, b, ca=1, cb=0):
    return lax.dot_general(a, b, (((ca,), (cb,)), ((), ())), preferred_element_type=F32)


def kernel(
    Z, PL, C, T, spread, feat,
    nodes_h, adj_h, gain_ref, w_in_h, w_out_h, cot_h,
    node_out_h, node_grad_h, gw_h, gg_h,
    nodes, w_in, w_out, cot, a2, x, x2,
    part, cin, acc, pin, full, part2, cin2, acc2, pin2, full2,
    gs, lh, rh, gpart, gin, gz, gzin, gw, gg, ggp, ggz, no_v, gg_v,
    loc, st, a_s, a_r, ar_s, ar_r, x_s, x_r, x2_s, x2_r,
    c_s, c_r, p_s, p_r, f_s, f_r, c2_s, c2_r, p2_s, p2_r, f2_s, f2_r,
    g_s, g_r, z_s, z_r, zg_s, zg_r, pg_s, pg_r, rg_s, rg_r,
    ggp_s, ggp_r, ggz_s, ggz_r,
):
    g = lax.axis_index("rows")
    r = lax.axis_index("rep")
    z, p = lax.div(g, PL), lax.rem(g, PL)
    ppr = Z // C
    group, D = nodes.shape
    pc = group // C
    rows_w = 2 * D // C // T
    w1 = rows_w // PL
    wz = w1 // Z if spread else w1
    zl = lax.rem(z, ppr)
    owner = lax.div(z, ppr) == r
    lead = r * ppr if feat else 0
    Dc = D // C
    my_cols = pl.ds(pl.multiple_of(r * Dc, Dc), Dc)
    sends = []
    stores = []

    def store(src, dst):
        c = pltpu.make_async_copy(src, dst, st.at[len(stores)])
        c.start()
        stores.append(c)

    def z_peer(d):
        return {"rows": lax.rem(z + d, Z) * PL + p}

    def p_peer(d):
        return {"rows": z * PL + lax.rem(p + d, PL)}

    def r_peer(d):
        return {"rep": lax.rem(r + d, C)}

    def rcopy(src, dst, ss, rs, dev):
        return pltpu.make_async_remote_copy(
            src_ref=src, dst_ref=dst, send_sem=ss, recv_sem=rs, device_id=dev, device_id_type=MESH
        )

    def send(src, dst, ss, rs, dev):
        c = rcopy(src, dst, ss, rs, dev)
        c.start()
        sends.append(c)

    def arrived(dst, ss, rs, dev):
        rcopy(dst, dst, ss, rs, dev).wait_recv()

    def cols_of(k):
        return pl.ds(pl.multiple_of((lead + k) * group, group), group)

    own_cols = [
        pltpu.make_async_copy(
            adj_h.at[:, pl.ds(pl.multiple_of((k * PL + p) * group, group), group)],
            a2.at[pl.ds(pl.multiple_of(p * group, group), group), cols_of(k)],
            loc.at[4 + k],
        )
        for k in range(ppr)
    ]
    loads = [
        pltpu.make_async_copy(cot_h, cot, loc.at[0]),
        pltpu.make_async_copy(w_out_h, w_out, loc.at[1]),
        pltpu.make_async_copy(w_in_h, w_in, loc.at[2]),
        pltpu.make_async_copy(nodes_h, nodes, loc.at[3]),
    ]
    loads[3].start()
    for c in own_cols:
        c.start()
    for c in loads[:3]:
        c.start()

    barrier = pltpu.get_barrier_semaphore()
    for n, peer in ((Z, z_peer), (PL, p_peer), (C, r_peer)):
        for d in range(1, n):
            pl.semaphore_signal(barrier, inc=1, device_id=peer(d), device_id_type=MESH)
    loads[3].wait()
    pl.semaphore_wait(barrier, Z + PL + C - 3)

    def z_rows(k):
        return pl.ds(pl.multiple_of(k * group, group), group)

    def z_copies(src, buf, ss, rs):
        if feat:
            slot = buf.at[z_rows(z)]
            return [
                rcopy(src.at[:, my_cols], slot, ss.at[d - 1], rs.at[d - 1], z_peer(d))
                for d in range(1, Z)
            ]
        slot = buf.at[pl.ds(pl.multiple_of(zl * group, group), group)]
        return [rcopy(src, slot, ss.at[d - 1], rs.at[zl], z_peer(d)) for d in range(1, Z)]

    def z_start(src, buf, ss, rs):
        if feat:
            for c in z_copies(src, buf, ss, rs):
                c.start()
            buf[z_rows(z)] = src[:, my_cols]
            return

        @pl.when(owner)
        def _():
            for c in z_copies(src, buf, ss, rs):
                c.start()
            buf[pl.ds(pl.multiple_of(zl * group, group), group)] = src[...]

    def z_wait(src, buf, ss, rs):
        if feat:
            for d in range(1, Z):
                slot = buf.at[z_rows(lax.rem(z + Z - d, Z))]
                arrived(slot, ss.at[d - 1], rs.at[d - 1], z_peer(d))
            return
        for k in range(ppr):
            @pl.when(r * ppr + k != z)
            def _():
                arrived(buf.at[pl.ds(k * group, group)], ss.at[0], rs.at[k], z_peer(1))

    def z_drain(src, buf, ss, rs):
        if feat:
            for c in z_copies(src, buf, ss, rs):
                c.wait_send()
            return

        @pl.when(owner)
        def _():
            for c in z_copies(src, buf, ss, rs):
                c.wait_send()

    z_start(nodes, x, x_s, x_r)
    for d in range(1, PL):
        q = lax.rem(p + d, PL)
        for k in range(ppr):
            send(
                adj_h.at[:, pl.ds(pl.multiple_of((k * PL + q) * group, group), group)],
                a2.at[pl.ds(pl.multiple_of(p * group, group), group), cols_of(k)],
                a_s.at[(d - 1) * ppr + k], a_r.at[(d - 1) * ppr + k], p_peer(d),
            )

    loads[0].wait()
    loads[1].wait()
    grad_hidden = dot(cot[...], w_out[...], 1, 1)
    loads[2].wait()
    for c in own_cols:
        c.wait()

    def halves(d, e):
        q = lax.rem(p + PL - d, PL)
        there = pl.multiple_of(lax.rem(r + C - e, C) * ppr * group, ppr * group)
        return a2.at[pl.ds(pl.multiple_of(q * group, group), group), pl.ds(there, ppr * group)]

    def forward(d):
        for e in range(1, C):
            i = d * (C - 1) + e - 1
            send(halves(d, 0), halves(d, 0), ar_s.at[i], ar_r.at[i], r_peer(e))

    if feat:
        forward(0)
    for d in range(1, PL):
        q = lax.rem(p + PL - d, PL)
        for k in range(ppr):
            arrived(
                a2.at[pl.ds(pl.multiple_of(q * group, group), group), cols_of(k)],
                a_s.at[(d - 1) * ppr + k], a_r.at[(d - 1) * ppr + k], p_peer(d),
            )
        if feat:
            forward(d)
    if feat:
        for d in range(PL):
            for e in range(1, C):
                i = d * (C - 1) + e - 1
                arrived(halves(d, e), ar_s.at[i], ar_r.at[i], r_peer(e))

    order = list(range(1, PL)) + [0]

    def partials(buf, out, ins, ss, rs):
        for d in order:
            q = lax.rem(p + d, PL)
            val = dot(a2[pl.ds(pl.multiple_of(q * group, group), group)], buf[...])
            for c in range(C):
                out[c, d] = val[c * pc:(c + 1) * pc].astype(out.dtype)
            for e in range(1, C):
                i = d * (C - 1) + e - 1
                send(out.at[lax.rem(r + e, C), d], ins.at[e - 1, d], ss.at[i], rs.at[i], r_peer(e))

    def combine(out, ins, ss, rs, accs, pins, pss, prs):
        for d in order:
            val = out[r, d].astype(F32)
            for e in range(1, C):
                i = d * (C - 1) + e - 1
                arrived(ins.at[e - 1, d], ss.at[i], rs.at[i], r_peer(e))
                val = val + ins[e - 1, d].astype(F32)
            if d == 0:
                return val
            accs[d - 1] = val.astype(accs.dtype)
            send(accs.at[d - 1], pins.at[d - 1], pss.at[d - 1], prs.at[d - 1], p_peer(d))

    def aggregate(buf, out, ins, ss, rs, accs, pins, pss, prs):
        if not feat:
            partials(buf, out, ins, ss, rs)
            return combine(out, ins, ss, rs, accs, pins, pss, prs)
        for d in order:
            q = lax.rem(p + d, PL)
            val = dot(a2[pl.ds(pl.multiple_of(q * group, group), group)], buf[...])
            if d == 0:
                return val
            accs[d - 1] = val.astype(accs.dtype)
            send(accs.at[d - 1], pins.at[d - 1], pss.at[d - 1], prs.at[d - 1], p_peer(d))

    def finish(val, accs, pins, pss, prs):
        for d in range(1, PL):
            arrived(pins.at[d - 1], pss.at[d - 1], prs.at[d - 1], p_peer(d))
            val = val + pins[d - 1].astype(F32)
        return val

    def piece_of(buf, c):
        if feat:
            return buf.at[:, pl.ds(pl.multiple_of(c * Dc, Dc), Dc)]
        return buf.at[pl.ds(pl.multiple_of(c * pc, pc), pc)]

    def share(buf, ss, rs):
        for d in range(1, C):
            send(piece_of(buf, r), piece_of(buf, r), ss.at[d - 1], rs.at[d - 1], r_peer(d))

    def shared(buf, ss, rs):
        for d in range(1, C):
            arrived(piece_of(buf, lax.rem(r + C - d, C)), ss.at[d - 1], rs.at[d - 1], r_peer(d))

    if feat:
        mine = (slice(None), my_cols)
    else:
        mine = pl.ds(pl.multiple_of(r * pc, pc), pc)
    z_wait(nodes, x, x_s, x_r)
    own = aggregate(x, part, cin, c_s, c_r, acc, pin, p_s, p_r)
    full[mine] = finish(own, acc, pin, p_s, p_r)
    share(full, f_s, f_r)
    shared(full, f_s, f_r)

    summed = full[...]
    gain = gain_ref[...]
    scale = lax.rsqrt(jnp.mean(summed * summed, axis=-1, keepdims=True) + 1e-05)
    normed = summed * scale
    lifted = (normed * gain).astype(BF16)
    pre = dot(lifted, w_in[...])
    sigma = jax.nn.sigmoid(pre)
    hidden = (pre * sigma).astype(BF16)

    def first_row(t, rep):
        if T == 1:
            return rep * rows_w
        return (1 - t) * D + rep * rows_w

    def weights_start(t, left, right):
        gval = dot(left, right, 0, 0)
        for q in range(PL):
            gpart[t, q] = gval[q * w1:(q + 1) * w1].astype(BF16)
        for d in range(1, PL):
            i = t * (PL - 1) + d - 1
            send(gpart.at[t, lax.rem(p + d, PL)], gin.at[i], g_s.at[i], g_r.at[i], p_peer(d))

    def columns(ref):
        return ref[:, pl.ds(pl.multiple_of(r * rows_w, rows_w), rows_w)]

    lh[1] = hidden
    grad_pre = (grad_hidden * sigma * (1.0 + pre * (1.0 - sigma))).astype(BF16)
    grad_lifted = dot(grad_pre, w_in[...], 1, 1)
    grad_normed = grad_lifted * gain
    gs[...] = (
        scale * (grad_normed - normed * jnp.mean(grad_normed * normed, axis=-1, keepdims=True))
    ).astype(BF16)
    z_start(gs, x2, x2_s, x2_r)

    lh[0] = lifted
    if T == 2:
        weights_start(0, columns(lh.at[1]), cot[...])
        weights_start(1, columns(lh.at[0]), grad_pre)
    else:
        rh[0] = grad_pre
        rh[1] = cot[...]
        half = C // 2
        which = lax.div(r, half)
        here = pl.multiple_of(lax.rem(r, half) * rows_w, rows_w)
        weights_start(0, lh[which, :, pl.ds(here, rows_w)], rh[which])
    gg[...] = jnp.broadcast_to(jnp.sum(grad_lifted * normed, axis=0, keepdims=True), gg.shape)
    ggp[p] = gg[...]
    for d in range(1, PL):
        send(gg, ggp.at[p], ggp_s.at[d - 1], ggp_r.at[d - 1], p_peer(d))
    no_v[...] = (nodes[...].astype(F32) + dot(hidden, w_out[...])).astype(BF16)
    store(no_v, node_out_h)

    def gw_rows(start, count):
        return gw.at[pl.ds(pl.multiple_of(start, count), count)]

    def scatter_z(t):
        gsum = gpart[t, p].astype(F32)
        for d in range(1, PL):
            i = t * (PL - 1) + d - 1
            arrived(gin.at[i], g_s.at[i], g_r.at[i], p_peer(d))
            gsum = gsum + gin[i].astype(F32)
        if spread:
            for k in range(Z):
                gz[t, k] = gsum[k * wz:(k + 1) * wz].astype(BF16)
        else:
            gz[t, 0] = gsum.astype(BF16)
            gzin[t, z] = gz[t, 0]
        for d in range(1, Z):
            i = t * (Z - 1) + d - 1
            src = gz.at[t, lax.rem(z + d, Z)] if spread else gz.at[t, 0]
            dst = gzin.at[t, d - 1] if spread else gzin.at[t, z]
            send(src, dst, z_s.at[i], z_r.at[i], z_peer(d))

    def gather_z(t):
        base = first_row(t, r) + p * w1
        shard = gz[t, z].astype(F32) if spread else None
        for d in range(1, Z):
            i = t * (Z - 1) + d - 1
            slot = gzin.at[t, d - 1] if spread else gzin.at[t, lax.rem(z + Z - d, Z)]
            arrived(slot, z_s.at[i], z_r.at[i], z_peer(d))
            if spread:
                shard = shard + gzin[t, d - 1].astype(F32)
        if not spread:
            shard = gzin[t, 0].astype(F32)
            for k in range(1, Z):
                shard = shard + gzin[t, k].astype(F32)
            gw[pl.ds(pl.multiple_of(base, w1), w1)] = shard.astype(BF16)
            return
        here = base + z * wz
        gw[pl.ds(pl.multiple_of(here, wz), wz)] = shard.astype(BF16)
        for d in range(1, Z):
            i = t * (Z - 1) + d - 1
            send(gw_rows(here, wz), gw_rows(here, wz), zg_s.at[i], zg_r.at[i], z_peer(d))

    def gather_plane(t):
        base = first_row(t, r) + p * w1
        if spread:
            for d in range(1, Z):
                i = t * (Z - 1) + d - 1
                there = base + lax.rem(z + Z - d, Z) * wz
                arrived(gw_rows(there, wz), zg_s.at[i], zg_r.at[i], z_peer(d))
        for d in range(1, PL):
            i = t * (PL - 1) + d - 1
            send(gw_rows(base, w1), gw_rows(base, w1), pg_s.at[i], pg_r.at[i], p_peer(d))

    def keep(start):
        store(gw_rows(start, w1), gw_h.at[pl.ds(pl.multiple_of(start, w1), w1)])

    def gather_rep(t):
        for d in range(PL):
            start = first_row(t, r) + lax.rem(p + PL - d, PL) * w1
            block = gw_rows(start, w1)
            if d > 0:
                i = t * (PL - 1) + d - 1
                arrived(block, pg_s.at[i], pg_r.at[i], p_peer(d))
            for e in range(1, C):
                i = (t * PL + d) * (C - 1) + e - 1
                send(block, block, rg_s.at[i], rg_r.at[i], r_peer(e))
            keep(start)

    def gather_end(t):
        for d in range(PL):
            for e in range(1, C):
                i = (t * PL + d) * (C - 1) + e - 1
                start = first_row(t, lax.rem(r + C - e, C)) + lax.rem(p + PL - d, PL) * w1
                arrived(gw_rows(start, w1), rg_s.at[i], rg_r.at[i], r_peer(e))
                keep(start)

    last = T - 1
    scatter_z(0)
    z_wait(gs, x2, x2_s, x2_r)
    own2 = aggregate(x2, part2, cin2, c2_s, c2_r, acc2, pin2, p2_s, p2_r)
    if T == 2:
        scatter_z(1)
        gather_z(0)
    gather_z(last)
    for t in range(T):
        gather_plane(t)

    for d in range(1, PL):
        arrived(ggp.at[lax.rem(p + PL - d, PL)], ggp_s.at[d - 1], ggp_r.at[d - 1], p_peer(d))
    ggv = ggp[0]
    for q in range(1, PL):
        ggv = ggv + ggp[q]
    ggz[z] = ggv
    for d in range(1, Z):
        send(ggz.at[z], ggz.at[z], ggz_s.at[d - 1], ggz_r.at[d - 1], z_peer(d))

    back = finish(own2, acc2, pin2, p2_s, p2_r)
    full2[mine] = (cot[mine].astype(F32) + back).astype(BF16)
    share(full2, f2_s, f2_r)
    gather_rep(0)
    shared(full2, f2_s, f2_r)
    store(full2, node_grad_h)
    if T == 2:
        gather_rep(1)
    for d in range(1, Z):
        arrived(ggz.at[lax.rem(z + Z - d, Z)], ggz_s.at[d - 1], ggz_r.at[d - 1], z_peer(d))
    ggv = ggz[0]
    for k in range(1, Z):
        ggv = ggv + ggz[k]
    gg_v[...] = ggv[:1]
    store(gg_v, gg_h)
    for t in range(T):
        gather_end(t)
    for c in sends:
        c.wait_send()
    z_drain(nodes, x, x_s, x_r)
    z_drain(gs, x2, x2_s, x2_r)
    for c in stores:
        c.wait()


def closing(
    chunks, node_out, node_grad, gw, gg, o_out, o_grad, o_win, o_wout, o_gain,
    narrow, wide, pair, gain, sem_in, sem_out,
):
    D = o_win.shape[0]
    rows = 2 * D // chunks
    cuts = [pl.ds(k * rows, rows) for k in range(chunks)]
    steps = [(gw.at[c], narrow.at[c]) for c in cuts]
    steps += [(node_out, pair.at[0]), (node_grad, pair.at[1]), (gg, gain)]
    loads = [pltpu.make_async_copy(a, b, sem_in.at[i]) for i, (a, b) in enumerate(steps)]
    for c in loads:
        c.start()
    outs = []
    for k in range(chunks):
        loads[k].wait()
        wide[cuts[k]] = narrow[cuts[k]].astype(F32)
        dst = o_win if k * rows < D else o_wout
        outs.append((wide.at[cuts[k]], dst.at[pl.ds(k * rows % D, rows)]))
        pltpu.make_async_copy(*outs[k], sem_out.at[k]).start()
    outs += [(pair.at[0], o_out), (pair.at[1], o_grad), (gain, o_gain)]
    for k in range(chunks, chunks + 3):
        loads[k].wait()
        pltpu.make_async_copy(*outs[k], sem_out.at[k]).start()
    for k in range(chunks + 3):
        pltpu.make_async_copy(*outs[k], sem_out.at[k]).wait()


def shards(Z, PL, C, nodes, adjacency, gain, w_in, w_out, cotangent):
    group, D = nodes.shape
    ppr = Z // C
    pc = group // C
    feat = D // C % 128 == 0
    T = 2 if D // C // PL % (16 * Z) == 0 else 1
    w1 = 2 * D // C // T // PL
    spread = w1 % (16 * Z) == 0
    wz = w1 // Z if spread else w1
    if feat:
        field, piece = (Z * group, D // C), (PL - 1, group, D // C)
        split = split_in = (8, 128)
    else:
        field, piece = (ppr * group, D), (PL - 1, pc, D)
        split, split_in = (C, PL, pc, D), (C - 1, PL, pc, D)
    V = pltpu.VMEM
    S = pltpu.SemaphoreType.DMA

    def pair(n):
        return [S((n,)), S((n,))]

    scratch = [
        V((group, D), BF16), V((D, D), BF16), V((D, D), BF16), V((group, D), BF16),
        *([V((PL * group, Z * group), BF16)] if feat else [V((PL * group, ppr * group), BF16)]),
        V(field, BF16), V(field, BF16),
        V(split, F32), V(split_in, F32), V(piece, BF16), V(piece, BF16), V((group, D), F32),
        V(split, BF16), V(split_in, BF16), V(piece, BF16), V(piece, BF16), V((group, D), BF16),
        V((group, D), BF16), V((2, group, D), BF16), V((2, group, D), BF16),
        V((T, PL, w1, D), BF16), V((T * (PL - 1), w1, D), BF16),
        V((T, Z if spread else 1, wz, D), BF16), V((T, Z - 1 if spread else Z, wz, D), BF16),
        V((2 * D, D), BF16),
        V((8, D), F32), V((PL, 8, D), F32), V((Z, 8, D), F32), V((group, D), BF16), V((1, D), F32),
        S((4 + ppr,)), S((3 + T * PL * C,)),
        *pair((PL - 1) * ppr), *pair(PL * (C - 1)),
        S((Z - 1,)), S((Z - 1,)), S((Z - 1,)), S((Z - 1,)),
        *pair(PL * (C - 1)), *pair(PL - 1), *pair(C - 1),
        *pair(PL * (C - 1)), *pair(PL - 1), *pair(C - 1),
        *pair(T * (PL - 1)), *pair(T * (Z - 1)), *pair(T * (Z - 1)), *pair(T * (PL - 1)),
        *pair(T * PL * (C - 1)),
        *pair(PL - 1), *pair(Z - 1),
    ]
    H = pl.BlockSpec(memory_space=pltpu.HBM)
    M = pl.BlockSpec(memory_space=pltpu.VMEM)
    parts = pl.pallas_call(
        functools.partial(kernel, Z, PL, C, T, spread, feat),
        out_shape=[
            jax.ShapeDtypeStruct((group, D), BF16),
            jax.ShapeDtypeStruct((group, D), BF16),
            jax.ShapeDtypeStruct((2 * D, D), BF16),
            jax.ShapeDtypeStruct((1, D), F32),
        ],
        in_specs=[H, H, M, H, H, H],
        out_specs=[H, H, H, H],
        scratch_shapes=scratch,
        compiler_params=pltpu.CompilerParams(
            collective_id=0, has_side_effects=True, vmem_limit_bytes=60 * 1024 * 1024
        ),
    )(nodes, adjacency, gain.reshape(1, D), w_in, w_out, cotangent)
    chunks = 8
    node_out, node_grad, g_in, g_out, gg = pl.pallas_call(
        functools.partial(closing, chunks),
        out_shape=[
            jax.ShapeDtypeStruct((group, D), BF16),
            jax.ShapeDtypeStruct((group, D), BF16),
            jax.ShapeDtypeStruct((D, D), F32),
            jax.ShapeDtypeStruct((D, D), F32),
            jax.ShapeDtypeStruct((1, D), F32),
        ],
        in_specs=[H, H, H, H],
        out_specs=[H, H, H, H, H],
        scratch_shapes=[
            V((2 * D, D), BF16), V((2 * D, D), F32), V((2, group, D), BF16), V((1, D), F32),
            S((chunks + 3,)), S((chunks + 3,)),
        ],
        compiler_params=pltpu.CompilerParams(vmem_limit_bytes=60 * 1024 * 1024),
    )(*parts)
    return node_out, node_grad, g_in, g_out, gg.reshape(D)


def solution(mesh):
    R, C = mesh.shape["rows"], mesh.shape["rep"]
    PL = math.isqrt(R)
    return jax.shard_map(
        functools.partial(shards, R // PL, PL, C),
        mesh=mesh,
        in_specs=(P("rows", None), P("rows", "rep"), P(), P(), P(), P("rows", None)),
        out_specs=(P("rows", None), P("rows", None), P(), P(), P()),
        check_vma=False,
    )
```
